32 devices in a mesh: ctx: 8 (over z, core), head: 4 (over y, x).
Axes of the slice: x: 2, y: 2, z: 4, core: 2. Of those that a mesh axis runs over, the one named last changes fastest.
Arguments:
- queries: bfloat16 [3072, 512], P(('ctx', 'head')), may hold values from -6 to 6
- keys: bfloat16 [3072, 512], P(('ctx', 'head')), may hold values from -6 to 6
- values: bfloat16 [3072, 512], P(('ctx', 'head')), may hold values from -6 to 6
- log_decay: bfloat16 [3072, 4], P(('ctx', 'head')), as said below
- gain: float32 [512], P('head'), may hold values from 0.1 to 1.9
- doc_starts: int32 [9], replicated, may hold values from 0 to 3072, as said below
Outputs:
- attended: bfloat16 [3072, 512], P(('ctx', 'head'))
The draws below stay inside these ranges and needn't reach their ends.
Inputs may be any that keep to these rules, and one draw needn't show every extreme that they name: doc_starts begins with 0, ends with 3072 and rises strictly; the first document holds at least 1920 tokens. `log_decay`: entries are at most 0.
All inputs are finite; a program needn't handle non-finite values.
Results may differ from the reference program's by a relative error of at most 0.0049.
Values may be sent and summed in bfloat16 or wider, within the bound.
A program may use at most 64 MiB of HBM per device.

```python
import math
import jax
import jax.numpy as jnp
from jax import lax

E = 128
H = 4
SEQUENCE_TOKENS = 3072
BLOCK = 384
NDOC = 8


def draw_log_decay(key, part):
    keys = jax.random.split(key, 6)
    fast_share = 0.5
    fast = jax.random.uniform(keys[0], (H,)) < fast_share
    fast_rate = 1.0 / jax.random.uniform(keys[1], (H,), minval=30.0, maxval=50.0)
    slow_factor = jnp.exp(jax.random.uniform(keys[2], (H,), minval=math.log(0.5), maxval=math.log(16.0)))
    slow_rate = math.log(2.0) / SEQUENCE_TOKENS * slow_factor
    decay_speed = jnp.where(fast, fast_rate, slow_rate)
    decay_multiplier = jnp.exp(jax.random.uniform(keys[3], (SEQUENCE_TOKENS, H), minval=math.log(0.5), maxval=math.log(2.0)))
    window_position = jax.random.randint(keys[4], (2,), 0, SEQUENCE_TOKENS)
    window_retained = jax.random.uniform(keys[5], (2,), minval=0.5, maxval=0.8)
    token_positions = jnp.arange(SEQUENCE_TOKENS, dtype=jnp.int32)
    decay_window = jnp.sum(jnp.where(token_positions[:, None] == window_position[None, :], jnp.log(window_retained)[None, :], 0.0), axis=1)
    return (-decay_speed[None, :] * decay_multiplier + decay_window[:, None]).astype(jnp.bfloat16)


def draw_doc_starts(key, part):
    lower = 5 * SEQUENCE_TOKENS // 8
    slot = (SEQUENCE_TOKENS - lower) // (NDOC - 1)
    offsets = jax.random.randint(key, (NDOC - 1,), 0, slot)
    inner = lower + jnp.arange(NDOC - 1, dtype=jnp.int32) * slot + offsets
    head_part = jnp.zeros((1,), jnp.int32)
    tail_part = jnp.full((1,), SEQUENCE_TOKENS, jnp.int32)
    return jnp.concatenate([head_part, inner.astype(jnp.int32), tail_part]).astype(jnp.int32)


def levels(own_key, extent, pieces, smallest, largest):
    loudness, own = 1.0, jax.random.fold_in(own_key, 6)
    for position, shards_of in pieces:
        draws = jnp.exp(jax.random.uniform(jax.random.fold_in(own, position), (shards_of,), jnp.float32, smallest / len(pieces), largest / len(pieces)))
        loudness = loudness * jnp.repeat(draws, extent[position] // shards_of).reshape([-1 if axis == position else 1 for axis in range(len(extent))])
    return loudness


def normal_values(rng, extent, width, limit, pieces=(), kind=jnp.bfloat16):
    drawn = width * jax.random.normal(rng, extent, jnp.float32)
    if pieces:
        drawn = drawn * levels(rng, extent, pieces, -0.22, 0.18)
    return jnp.clip(drawn, -limit, limit).astype(kind)


def setup_inputs(seed: int = 0) -> dict:
    seeds = jax.random.split(jax.random.key(seed), 7)
    return {
        "queries": normal_values(seeds[0], (SEQUENCE_TOKENS, H * E), 1.0, 6.0, ((0, 32),)),
        "keys": normal_values(seeds[1], (SEQUENCE_TOKENS, H * E), 1.0, 6.0, ((0, 32),)),
        "values": normal_values(seeds[2], (SEQUENCE_TOKENS, H * E), 1.0, 6.0, ((0, 32),)),
        "log_decay": draw_log_decay(jax.random.fold_in(seeds[6], 71), 0),
        "gain": jnp.clip(1.0 + 0.18 * jax.random.normal(seeds[4], (H * E,), jnp.float32), 0.1, 1.9),
        "doc_starts": draw_doc_starts(jax.random.fold_in(seeds[6], 71), 0),
    }


def reference(queries, keys, values, log_decay, gain, doc_starts):
    nblk = SEQUENCE_TOKENS // BLOCK
    token_positions = jnp.arange(SEQUENCE_TOKENS, dtype=jnp.int32)
    doc_id = lax.optimization_barrier(jnp.sum((token_positions[:, None] >= doc_starts[None, 1:NDOC]).astype(jnp.int32), axis=1))
    is_start = jnp.any(token_positions[:, None] == doc_starts[None, 0:NDOC], axis=1)
    qb = queries.reshape(nblk, BLOCK, H, E)
    kb = keys.reshape(nblk, BLOCK, H, E)
    vb = values.reshape(nblk, BLOCK, H, E)
    gb = log_decay.reshape(nblk, BLOCK, H)
    docb = doc_id.reshape(nblk, BLOCK)
    startb = is_start.reshape(nblk, BLOCK)
    gain_heads = gain.reshape(H, E)
    rows = jnp.arange(BLOCK, dtype=jnp.int32)

    def step(state, item):
        qx, kx, vx, gx, dx, sx = item
        cum = jnp.cumsum(gx.astype(jnp.float32), axis=0)
        opened = jnp.cumsum(sx.astype(jnp.int32)) == 0
        mask = (rows[None, :] <= rows[:, None]) & (dx[:, None] == dx[None, :])
        cum_t = cum.T
        diff = cum_t[:, :, None] - cum_t[:, None, :]
        decay = jnp.where(mask[None], jnp.exp(jnp.where(mask[None], diff, 0.0)), 0.0)
        scores = jnp.einsum('thd,jhd->htj', qx.astype(jnp.float32), kx.astype(jnp.float32))
        weights = (scores * decay).astype(jnp.bfloat16)
        intra = jnp.einsum('htj,jhe->the', weights.astype(jnp.float32), vx.astype(jnp.float32))
        reach = jnp.exp(cum) * opened[:, None].astype(jnp.float32)
        scaled_q = qx.astype(jnp.float32) * reach[:, :, None]
        inter = jnp.einsum('the,hef->thf', scaled_q, state, precision=lax.Precision.HIGHEST)
        attn = intra + inter
        meansq = lax.optimization_barrier(jnp.mean(attn * attn, axis=-1, keepdims=True))
        normed = attn * lax.rsqrt(meansq + 1e-05) * gain_heads[None]
        last = cum[-1]
        tail = jnp.exp(last[None, :] - cum) * (dx == dx[-1])[:, None].astype(jnp.float32)
        scaled_keys = (kx.astype(jnp.float32) * tail[:, :, None]).astype(jnp.bfloat16)
        summary = jnp.einsum('jhe,jhf->hef', scaled_keys.astype(jnp.float32), vx.astype(jnp.float32))
        keep = jnp.exp(last) * opened[-1].astype(jnp.float32)
        state = keep[:, None, None] * state + summary
        return (state, normed.astype(jnp.bfloat16).reshape(BLOCK, H * E))
    init = jnp.zeros((H, E, E), jnp.float32)
    final_state, outs = lax.scan(step, init, (qb, kb, vb, gb, docb, startb))
    return outs.reshape(SEQUENCE_TOKENS, H * E)
```

```python
import functools

import jax
import jax.numpy as jnp
from jax import lax
from jax.experimental import pallas as pl
from jax.experimental.pallas import tpu as pltpu
from jax.sharding import PartitionSpec as P

E = 128


block_cap = 512


def carried_in(value, axis, join, neutral):
    count, mine = (lax.axis_size(axis), lax.axis_index(axis))
    pieces = jax.tree.map(lambda part: lax.all_gather(part, axis), value)
    total = jax.tree.map(
        lambda part, zero: jnp.full_like(part, 0) + jnp.asarray(zero, part.dtype), value, neutral
    )

    def hop(position, total):
        longer = join(total, jax.tree.map(lambda part: part[position], pieces))
        return jax.tree.map(lambda new, old: jnp.where(position < mine, new, old), longer, total)

    return lax.fori_loop(0, count - 1, hop, total)


def combine(earlier, later):
    return (earlier[0] * later[0], later[0][:, None, None] * earlier[1] + later[1])


def scanned(queries, keys, values, log_decay, gain, doc_starts):
    heads = gain.shape[0] // E
    q_group = lax.all_to_all(queries, "head", split_axis=1, concat_axis=0, tiled=True)
    k_group, v_group, g_group = (
        lax.all_to_all(keys, "head", split_axis=1, concat_axis=0, tiled=True),
        lax.all_to_all(values, "head", split_axis=1, concat_axis=0, tiled=True),
        lax.all_to_all(log_decay, "head", split_axis=1, concat_axis=0, tiled=True),
    )
    group = q_group.shape[0]
    block = min(block_cap, group)
    nblk = group // block
    ndoc = doc_starts.shape[0] - 1
    offset = lax.axis_index("ctx") * group
    token_positions = offset + jnp.arange(group, dtype=jnp.int32)
    doc_id = jnp.sum(
        (token_positions[:, None] >= doc_starts[None, 1:ndoc]).astype(jnp.int32), axis=1
    )
    is_start = jnp.any(token_positions[:, None] == doc_starts[None, 0:ndoc], axis=1)
    qb = q_group.reshape(nblk, block, heads, E)
    kb = k_group.reshape(nblk, block, heads, E)
    vb = v_group.reshape(nblk, block, heads, E)
    gb = g_group.reshape(nblk, block, heads)
    docb = doc_id.reshape(nblk, block)
    startb = is_start.reshape(nblk, block)
    rows = jnp.arange(block, dtype=jnp.int32)

    def local_block(carry, item):
        acc_a, acc_s = carry
        qx, kx, vx, gx, dx, sx = item
        cum = jnp.cumsum(gx.astype(jnp.float32), axis=0)
        opened = jnp.cumsum(sx.astype(jnp.int32)) == 0
        mask = (rows[None, :] <= rows[:, None]) & (dx[:, None] == dx[None, :])
        cum_t = cum.T
        diff = cum_t[:, :, None] - cum_t[:, None, :]
        decay = jnp.where(mask[None], jnp.exp(jnp.where(mask[None], diff, 0.0)), 0.0)
        scores = jnp.einsum("thd,jhd->htj", qx, kx, preferred_element_type=jnp.float32)
        weights = (scores * decay).astype(jnp.bfloat16)
        intra = jnp.einsum("htj,jhe->the", weights, vx, preferred_element_type=jnp.float32)
        last = cum[-1]
        tail = jnp.exp(last[None, :] - cum) * (dx == dx[-1])[:, None].astype(jnp.float32)
        scaled_keys = (kx.astype(jnp.float32) * tail[:, :, None]).astype(jnp.bfloat16)
        summary = jnp.einsum("jhe,jhf->hef", scaled_keys, vx, preferred_element_type=jnp.float32)
        keep = jnp.exp(last) * opened[-1].astype(jnp.float32)
        reach = jnp.exp(cum) * opened[:, None].astype(jnp.float32)
        updated = (acc_a * keep, keep[:, None, None] * acc_s + summary)
        return (updated, (intra, reach, acc_a, acc_s))

    start_carry = (jnp.ones((heads,), jnp.float32), jnp.zeros((heads, E, E), jnp.float32))
    device_sum, stacked = lax.scan(local_block, start_carry, (qb, kb, vb, gb, docb, startb))
    intra, reach, pre_a, pre_s = stacked
    dev_a, dev_s = device_sum
    enter_a, enter_s = carried_in((dev_a, dev_s), "ctx", combine, start_carry)
    block_in = pre_a[:, :, None, None] * enter_s[None] + pre_s
    scaled_q = qb.astype(jnp.float32) * reach[..., None]
    inter = jnp.einsum("bthe,bhef->bthf", scaled_q, block_in, precision=lax.Precision.HIGHEST)
    attn = intra + inter
    meansq = jnp.mean(attn * attn, axis=-1, keepdims=True)
    normed = attn * lax.rsqrt(meansq + 1e-05) * gain.reshape(heads, E)[None, None]
    result = normed.astype(jnp.bfloat16).reshape(group, heads * E)
    return lax.all_to_all(result, "head", split_axis=0, concat_axis=1, tiled=True)


KEEP_ROWS = 16
F32, BF16 = jnp.float32, jnp.bfloat16


def dot(a, b, dims=((1,), (0,))):
    return lax.dot_general(a, b, (dims, ((), ())), preferred_element_type=F32)


def split3(x):
    hi = x.astype(BF16).astype(F32)
    mid = (x - hi).astype(BF16).astype(F32)
    return hi, mid, x - hi - mid


def put_message(ref, state, keep):
    hi, mid, low = split3(jnp.broadcast_to(keep, (KEEP_ROWS, E)))
    row = lax.broadcasted_iota(jnp.int32, (KEEP_ROWS, E), 0)
    zero = jnp.zeros_like(hi)
    rows = jnp.where(row == 0, hi, jnp.where(row == 1, mid, jnp.where(row == 2, low, zero)))
    ref[pl.ds(0, E), :] = state.astype(BF16)
    ref[pl.ds(E, KEEP_ROWS), :] = rows.astype(BF16)


def get_message(ref):
    state = ref[pl.ds(0, E), :].astype(F32)
    keep = jnp.sum(ref[pl.ds(E, KEEP_ROWS), :].astype(F32), axis=0, keepdims=True)
    return state, keep


def fused(
    nh, nchip, q_ref, k_ref, v_ref, g_ref, gain_ref, ds_ref, o_ref,
    qs, ks, vs, gs, gain_s, mine_m, pair_m, chip_m, chip_in, enter, factor, osend,
    own_sem, send_sem, recv_sem, pair_sem, chip_send, chip_recv, out_send, out_recv,
):
    ctx, head = lax.axis_index("ctx"), lax.axis_index("head")
    tokens = k_ref.shape[0]
    group = tokens * nh
    chip, core = ctx // 2, ctx % 2
    sibling = ctx + 1 - 2 * core
    mesh_id = pl.DeviceIdType.MESH

    def columns(h):
        return pl.ds(pl.multiple_of(h * E, E), E)

    def quarter(h):
        return pl.ds(pl.multiple_of(h * tokens, tokens), tokens)

    arrays = ((g_ref, gs), (k_ref, ks), (v_ref, vs), (q_ref, qs))

    def piece(a, h):
        return arrays[a][0] if a == 0 else arrays[a][0].at[:, columns(h)]

    own = [
        pltpu.make_async_copy(piece(a, head), arrays[a][1].at[quarter(head)], own_sem.at[a])
        for a in range(4)
    ]
    own.append(pltpu.make_async_copy(gain_ref, gain_s, own_sem.at[4]))
    for copy in own:
        copy.start()

    barrier = pltpu.get_barrier_semaphore()
    partners = [(ctx, lax.rem(head + d, nh)) for d in range(1, nh)] + [(sibling, head)]
    partners += [(lax.rem(chip + d, nchip) * 2 + core, head) for d in range(1, nchip)]
    for partner in partners:
        pl.semaphore_signal(barrier, inc=1, device_id=partner, device_id_type=mesh_id)
    pl.semaphore_wait(barrier, len(partners))

    sends = {}
    for a in range(4):
        for d in range(1, nh):
            peer = lax.rem(head + d, nh)
            sends[a, d] = pltpu.make_async_remote_copy(
                src_ref=piece(a, peer),
                dst_ref=arrays[a][1].at[quarter(head)],
                send_sem=send_sem.at[a, d - 1],
                recv_sem=recv_sem.at[a, d - 1],
                device_id=(ctx, peer),
                device_id_type=mesh_id,
            )
            sends[a, d].start()

    def arrived(a):
        own[a].wait()
        for d in range(1, nh):
            sends[a, d].wait_recv()

    offset = ctx * group
    ndoc = ds_ref.shape[0] - 1
    last_token = offset + group - 1
    t_pos = offset + lax.broadcasted_iota(jnp.int32, (group, E), 0)
    begun = jnp.zeros((group, E), jnp.int32)
    begun_last = jnp.int32(0)
    for m in range(ndoc):
        s = ds_ref[m]
        begun = jnp.where(t_pos >= s, s, begun)
        begun_last = jnp.where(last_token >= s, s, begun_last)
    t_wide = lax.broadcasted_iota(jnp.int32, (group, group), 0)
    j_wide = lax.broadcasted_iota(jnp.int32, (group, group), 1)
    lower = jnp.where(t_wide >= j_wide, 1.0, 0.0).astype(BF16)
    upper = jnp.where(j_wide > t_wide, 1.0, 0.0).astype(BF16)
    later = jnp.where(t_wide > j_wide, 1.0, 0.0)

    arrived(0)
    lane = lax.broadcasted_iota(jnp.int32, gs.shape, 1)
    g = jnp.sum(jnp.where(lane == head, gs[...].astype(F32), 0.0), axis=1, keepdims=True)
    g_lanes = jnp.broadcast_to(g, (group, E)).astype(BF16)
    cum = dot(lower, g_lanes)
    to_end = dot(upper, g_lanes)
    reach = jnp.exp(cum) * jnp.where(begun < offset, 1.0, 0.0)
    tail = jnp.exp(to_end) * jnp.where(t_pos >= begun_last, 1.0, 0.0)
    keep = reach[group - 1 :, :]

    arrived(1)
    scaled = (ks[...].astype(F32) * tail).astype(BF16)
    arrived(2)
    summary = dot(scaled, vs[...], ((0,), (0,)))
    put_message(mine_m, summary, keep)
    to_pair = pltpu.make_async_remote_copy(
        src_ref=mine_m, dst_ref=pair_m, send_sem=pair_sem.at[0], recv_sem=pair_sem.at[1],
        device_id=(sibling, head), device_id_type=mesh_id,
    )
    to_pair.start()

    between = dot(lower, (later * g).astype(BF16))
    allowed = (j_wide <= t_wide) & (j_wide + offset >= begun[:, :1])
    decay = jnp.where(allowed, jnp.exp(between), 0.0)

    to_pair.wait_recv()
    pair_state, pair_keep = get_message(pair_m)
    first_core = core == 0
    total = jnp.where(
        first_core, pair_keep * summary + pair_state, keep * pair_state + summary
    )
    put_message(chip_m, total, pair_keep * keep)

    def to_chip(d):
        return pltpu.make_async_remote_copy(
            src_ref=chip_m, dst_ref=chip_in.at[d - 1],
            send_sem=chip_send.at[d - 1], recv_sem=chip_recv.at[d - 1],
            device_id=(lax.rem(chip + d, nchip) * 2 + core, head), device_id_type=mesh_id,
        )

    for d in range(1, nchip):
        @pl.when(chip + d < nchip)
        def _():
            to_chip(d).start()

    arrived(3)
    scores = dot(qs[...], ks[...], ((1,), (1,)))
    attn = dot((scores * decay).astype(BF16), vs[...])

    enter[...] = jnp.zeros_like(enter)
    factor[...] = jnp.ones_like(factor)
    for d in range(1, nchip):
        @pl.when(chip >= d)
        def _():
            to_chip(d).wait_recv()
            state, held = get_message(chip_in.at[d - 1])
            enter[...] += factor[...] * state
            factor[...] = factor[...] * held
    state = enter[...]
    state = jnp.where(first_core, state, pair_keep * state + pair_state)
    hi = state.astype(BF16)
    low = (state - hi.astype(F32)).astype(BF16)
    attn += reach * (dot(qs[...], hi) + dot(qs[...], low))
    own[4].wait()
    meansq = jnp.mean(attn * attn, axis=1, keepdims=True)
    osend[...] = (attn * lax.rsqrt(meansq + 1e-05) * gain_s[...]).astype(BF16)

    back = []
    for d in range(1, nh):
        peer = lax.rem(head + d, nh)
        copy = pltpu.make_async_remote_copy(
            src_ref=osend.at[quarter(peer)], dst_ref=o_ref.at[:, columns(head)],
            send_sem=out_send.at[d - 1], recv_sem=out_recv.at[d - 1],
            device_id=(ctx, peer), device_id_type=mesh_id,
        )
        copy.start()
        back.append(copy)
    home = pltpu.make_async_copy(
        osend.at[quarter(head)], o_ref.at[:, columns(head)], own_sem.at[5]
    )
    home.start()

    to_pair.wait_send()
    for copy in sends.values():
        copy.wait_send()
    for d in range(1, nchip):
        @pl.when(chip + d < nchip)
        def _():
            to_chip(d).wait_send()
    home.wait()
    for copy in back:
        copy.wait()


def fused_device(queries, keys, values, log_decay, gain, doc_starts):
    nh, nctx = lax.axis_size("head"), lax.axis_size("ctx")
    nchip = nctx // 2
    tokens = queries.shape[0]
    group = tokens * nh
    hbm = pl.BlockSpec(memory_space=pl.ANY)
    dma = pltpu.SemaphoreType.DMA
    return pl.pallas_call(
        functools.partial(fused, nh, nchip),
        out_shape=jax.ShapeDtypeStruct(queries.shape, queries.dtype),
        in_specs=[hbm] * 5 + [pl.BlockSpec(memory_space=pltpu.SMEM)],
        out_specs=hbm,
        scratch_shapes=[
            pltpu.VMEM((group, E), BF16),
            pltpu.VMEM((group, E), BF16),
            pltpu.VMEM((group, E), BF16),
            pltpu.VMEM((group, log_decay.shape[1]), BF16),
            pltpu.VMEM((1, E), F32),
            pltpu.VMEM((E + KEEP_ROWS, E), BF16),
            pltpu.VMEM((E + KEEP_ROWS, E), BF16),
            pltpu.VMEM((E + KEEP_ROWS, E), BF16),
            pltpu.VMEM((max(nchip - 1, 1), E + KEEP_ROWS, E), BF16),
            pltpu.VMEM((E, E), F32),
            pltpu.VMEM((1, E), F32),
            pltpu.VMEM((group, E), BF16),
            dma((6,)),
            dma((4, nh - 1)),
            dma((4, nh - 1)),
            dma((2,)),
            dma((max(nchip - 1, 1),)),
            dma((max(nchip - 1, 1),)),
            dma((nh - 1,)),
            dma((nh - 1,)),
        ],
        compiler_params=pltpu.CompilerParams(
            collective_id=0, has_side_effects=True, vmem_limit_bytes=32 * 1024 * 1024
        ),
        cost_estimate=pl.CostEstimate(
            flops=2 * group * E * (2 * group + 3 * E) + 2 * group**3,
            bytes_accessed=8 * group * E,
            transcendentals=group * group,
        ),
    )(queries, keys, values, log_decay, gain.reshape(1, E), doc_starts)


def per_device(queries, keys, values, log_decay, gain, doc_starts):
    nh, nctx = lax.axis_size("head"), lax.axis_size("ctx")
    tokens = queries.shape[0]
    one_block = tokens * nh <= block_cap and tokens % 16 == 0
    if one_block and gain.shape[0] == E and nh > 1 and nctx % 2 == 0:
        return fused_device(queries, keys, values, log_decay, gain, doc_starts)
    return scanned(queries, keys, values, log_decay, gain, doc_starts)


def solution(mesh):
    in_specs = (
        P(("ctx", "head"), None),
        P(("ctx", "head"), None),
        P(("ctx", "head"), None),
        P(("ctx", "head"), None),
        P("head"),
        P(),
    )
    out_specs = P(("ctx", "head"), None)
    return jax.shard_map(
        per_device, mesh=mesh, in_specs=in_specs, out_specs=out_specs, check_vma=False
    )
```

```python
import functools

import jax
import jax.numpy as jnp
from jax import lax
from jax.experimental import pallas as pl
from jax.experimental.pallas import tpu as pltpu
from jax.sharding import PartitionSpec as P

E = 128


block_cap = 512


def carried_in(value, axis, join, neutral):
    count, mine = (lax.axis_size(axis), lax.axis_index(axis))
    pieces = jax.tree.map(lambda part: lax.all_gather(part, axis), value)
    total = jax.tree.map(
        lambda part, zero: jnp.full_like(part, 0) + jnp.asarray(zero, part.dtype), value, neutral
    )

    def hop(position, total):
        longer = join(total, jax.tree.map(lambda part: part[position], pieces))
        return jax.tree.map(lambda new, old: jnp.where(position < mine, new, old), longer, total)

    return lax.fori_loop(0, count - 1, hop, total)


def combine(earlier, later):
    return (earlier[0] * later[0], later[0][:, None, None] * earlier[1] + later[1])


def scanned(queries, keys, values, log_decay, gain, doc_starts):
    heads = gain.shape[0] // E
    q_group = lax.all_to_all(queries, "head", split_axis=1, concat_axis=0, tiled=True)
    k_group, v_group, g_group = (
        lax.all_to_all(keys, "head", split_axis=1, concat_axis=0, tiled=True),
        lax.all_to_all(values, "head", split_axis=1, concat_axis=0, tiled=True),
        lax.all_to_all(log_decay, "head", split_axis=1, concat_axis=0, tiled=True),
    )
    group = q_group.shape[0]
    block = min(block_cap, group)
    nblk = group // block
    ndoc = doc_starts.shape[0] - 1
    offset = lax.axis_index("ctx") * group
    token_positions = offset + jnp.arange(group, dtype=jnp.int32)
    doc_id = jnp.sum(
        (token_positions[:, None] >= doc_starts[None, 1:ndoc]).astype(jnp.int32), axis=1
    )
    is_start = jnp.any(token_positions[:, None] == doc_starts[None, 0:ndoc], axis=1)
    qb = q_group.reshape(nblk, block, heads, E)
    kb = k_group.reshape(nblk, block, heads, E)
    vb = v_group.reshape(nblk, block, heads, E)
    gb = g_group.reshape(nblk, block, heads)
    docb = doc_id.reshape(nblk, block)
    startb = is_start.reshape(nblk, block)
    rows = jnp.arange(block, dtype=jnp.int32)

    def local_block(carry, item):
        acc_a, acc_s = carry
        qx, kx, vx, gx, dx, sx = item
        cum = jnp.cumsum(gx.astype(jnp.float32), axis=0)
        opened = jnp.cumsum(sx.astype(jnp.int32)) == 0
        mask = (rows[None, :] <= rows[:, None]) & (dx[:, None] == dx[None, :])
        cum_t = cum.T
        diff = cum_t[:, :, None] - cum_t[:, None, :]
        decay = jnp.where(mask[None], jnp.exp(jnp.where(mask[None], diff, 0.0)), 0.0)
        scores = jnp.einsum("thd,jhd->htj", qx, kx, preferred_element_type=jnp.float32)
        weights = (scores * decay).astype(jnp.bfloat16)
        intra = jnp.einsum("htj,jhe->the", weights, vx, preferred_element_type=jnp.float32)
        last = cum[-1]
        tail = jnp.exp(last[None, :] - cum) * (dx == dx[-1])[:, None].astype(jnp.float32)
        scaled_keys = (kx.astype(jnp.float32) * tail[:, :, None]).astype(jnp.bfloat16)
        summary = jnp.einsum("jhe,jhf->hef", scaled_keys, vx, preferred_element_type=jnp.float32)
        keep = jnp.exp(last) * opened[-1].astype(jnp.float32)
        reach = jnp.exp(cum) * opened[:, None].astype(jnp.float32)
        updated = (acc_a * keep, keep[:, None, None] * acc_s + summary)
        return (updated, (intra, reach, acc_a, acc_s))

    start_carry = (jnp.ones((heads,), jnp.float32), jnp.zeros((heads, E, E), jnp.float32))
    device_sum, stacked = lax.scan(local_block, start_carry, (qb, kb, vb, gb, docb, startb))
    intra, reach, pre_a, pre_s = stacked
    dev_a, dev_s = device_sum
    enter_a, enter_s = carried_in((dev_a, dev_s), "ctx", combine, start_carry)
    block_in = pre_a[:, :, None, None] * enter_s[None] + pre_s
    scaled_q = qb.astype(jnp.float32) * reach[..., None]
    inter = jnp.einsum("bthe,bhef->bthf", scaled_q, block_in, precision=lax.Precision.HIGHEST)
    attn = intra + inter
    meansq = jnp.mean(attn * attn, axis=-1, keepdims=True)
    normed = attn * lax.rsqrt(meansq + 1e-05) * gain.reshape(heads, E)[None, None]
    result = normed.astype(jnp.bfloat16).reshape(group, heads * E)
    return lax.all_to_all(result, "head", split_axis=0, concat_axis=1, tiled=True)


KEEP_ROWS = 16
F32, BF16 = jnp.float32, jnp.bfloat16


def dot(a, b, dims=((1,), (0,))):
    return lax.dot_general(a, b, (dims, ((), ())), preferred_element_type=F32)


def split3(x):
    hi = x.astype(BF16).astype(F32)
    mid = (x - hi).astype(BF16).astype(F32)
    return hi, mid, x - hi - mid


def put_message(ref, state, keep):
    hi, mid, low = split3(jnp.broadcast_to(keep, (KEEP_ROWS, E)))
    row = lax.broadcasted_iota(jnp.int32, (KEEP_ROWS, E), 0)
    zero = jnp.zeros_like(hi)
    rows = jnp.where(row == 0, hi, jnp.where(row == 1, mid, jnp.where(row == 2, low, zero)))
    ref[pl.ds(0, E), :] = state.astype(BF16)
    ref[pl.ds(E, KEEP_ROWS), :] = rows.astype(BF16)


def get_message(ref):
    state = ref[pl.ds(0, E), :].astype(F32)
    keep = jnp.sum(ref[pl.ds(E, KEEP_ROWS), :].astype(F32), axis=0, keepdims=True)
    return state, keep


def fused(
    nh, nchip, q_ref, k_ref, v_ref, g_ref, gain_ref, ds_hbm, o_ref,
    ql, kl, vl, gl, ds_ref, qs, ks, vs, gs, gain_s, lower_s, later_s, decay_s, gcol,
    mine_m, pair_m, chip_m, chip_in, enter, factor, attn_s, osend,
    own_sem, send_sem, recv_sem, pair_sem, chip_send, chip_recv, out_send, out_recv,
):
    ctx, head = lax.axis_index("ctx"), lax.axis_index("head")
    tokens = k_ref.shape[0]
    group = tokens * nh
    chunk = E if group % E == 0 else group
    chunks = [(i * chunk, (i + 1) * chunk) for i in range(group // chunk)]
    chip, core = ctx // 2, ctx % 2
    sibling = ctx + 1 - 2 * core
    mesh_id = pl.DeviceIdType.MESH

    def columns(h):
        return pl.ds(pl.multiple_of(h * E, E), E)

    def quarter(h):
        return pl.ds(pl.multiple_of(h * tokens, tokens), tokens)

    local = (gl, kl, vl, ql)
    loads = [
        pltpu.make_async_copy(ref, buf, own_sem.at[a])
        for a, (ref, buf) in enumerate(zip((g_ref, k_ref, v_ref, q_ref), local))
    ]
    loads.append(pltpu.make_async_copy(gain_ref, gain_s, own_sem.at[4]))
    loads.append(pltpu.make_async_copy(ds_hbm, ds_ref, own_sem.at[5]))
    for copy in loads:
        copy.start()

    barrier = pltpu.get_barrier_semaphore()
    partners = [(ctx, lax.rem(head + d, nh)) for d in range(1, nh)] + [(sibling, head)]
    partners += [(lax.rem(chip + d, nchip) * 2 + core, head) for d in range(1, nchip)]
    for partner in partners:
        pl.semaphore_signal(barrier, inc=1, device_id=partner, device_id_type=mesh_id)

    t_wide = lax.broadcasted_iota(jnp.int32, (group, group), 0)
    j_wide = lax.broadcasted_iota(jnp.int32, (group, group), 1)
    lower_s[...] = jnp.where(t_wide >= j_wide, 1.0, 0.0).astype(BF16)
    later_s[...] = jnp.where(t_wide > j_wide, 1.0, 0.0)

    for a in range(4):
        loads[a].wait()
    pl.semaphore_wait(barrier, len(partners))

    places = (gs, ks, vs, qs)

    def piece(a, h):
        return gl if a == 0 else local[a].at[:, columns(h)]

    def place(a, h):
        return gs.at[h] if a == 0 else places[a].at[quarter(h)]

    sends = {}
    for a in range(4):
        for d in range(1, nh):
            peer = lax.rem(head + d, nh)
            sends[a, d] = pltpu.make_async_remote_copy(
                src_ref=piece(a, peer), dst_ref=place(a, head),
                send_sem=send_sem.at[a, d - 1], recv_sem=recv_sem.at[a, d - 1],
                device_id=(ctx, peer), device_id_type=mesh_id,
            )
            sends[a, d].start()
    own = [
        pltpu.make_async_copy(piece(a, head), place(a, head), own_sem.at[6 + a])
        for a in range(4)
    ]
    for copy in own:
        copy.start()

    def arrived(a):
        own[a].wait()
        for d in range(1, nh):
            sends[a, d].wait_recv()

    loads[4].wait()
    loads[5].wait()
    offset = ctx * group
    ndoc = ds_ref.shape[0] - 1
    last_token = offset + group - 1
    t_pos = offset + lax.broadcasted_iota(jnp.int32, (group, E), 0)
    begun = jnp.zeros((group, E), jnp.int32)
    begun_last = jnp.int32(0)
    for m in range(ndoc):
        s = ds_ref[m]
        begun = jnp.where(t_pos >= s, s, begun)
        begun_last = jnp.where(last_token >= s, s, begun_last)

    arrived(0)
    ones = jnp.ones((gs.shape[1], E), BF16)
    row = lax.broadcasted_iota(jnp.int32, gs.shape[1:], 0)
    for t in range(nh):
        rows = jnp.where(row == head, gs[t].astype(F32), 0.0).astype(BF16)
        gcol[pl.ds(t * tokens, tokens), :] = dot(rows, ones, ((0,), (0,)))
    g_lanes = gcol[...]
    cum = dot(lower_s[...], g_lanes.astype(BF16))
    reach = jnp.exp(cum) * jnp.where(begun < offset, 1.0, 0.0)
    tail = jnp.exp(cum[group - 1 :, :] - cum) * jnp.where(t_pos >= begun_last, 1.0, 0.0)
    keep = reach[group - 1 :, :]
    for lo, hi in chunks:
        steps = (later_s[:hi, :hi] * g_lanes[:hi, :1]).astype(BF16)
        between = dot(lower_s[lo:hi, :hi], steps)
        t_at = lo + lax.broadcasted_iota(jnp.int32, (hi - lo, hi), 0)
        j_at = lax.broadcasted_iota(jnp.int32, (hi - lo, hi), 1)
        allowed = (j_at <= t_at) & (j_at + offset >= begun[lo:hi, :1])
        decay_s[lo:hi, :hi] = jnp.where(allowed, jnp.exp(between), 0.0)

    arrived(1)
    scaled = (ks[...].astype(F32) * tail).astype(BF16)
    arrived(2)
    summary = dot(scaled, vs[...], ((0,), (0,)))
    put_message(mine_m, summary, keep)
    to_pair = pltpu.make_async_remote_copy(
        src_ref=mine_m, dst_ref=pair_m, send_sem=pair_sem.at[0], recv_sem=pair_sem.at[1],
        device_id=(sibling, head), device_id_type=mesh_id,
    )
    to_pair.start()

    to_pair.wait_recv()
    pair_state, pair_keep = get_message(pair_m)
    first_core = core == 0
    total = jnp.where(
        first_core, pair_keep * summary + pair_state, keep * pair_state + summary
    )
    put_message(chip_m, total, pair_keep * keep)

    def to_chip(d):
        return pltpu.make_async_remote_copy(
            src_ref=chip_m, dst_ref=chip_in.at[d - 1],
            send_sem=chip_send.at[d - 1], recv_sem=chip_recv.at[d - 1],
            device_id=(lax.rem(chip + d, nchip) * 2 + core, head), device_id_type=mesh_id,
        )

    for d in range(1, nchip):
        @pl.when(chip + d < nchip)
        def _():
            to_chip(d).start()

    arrived(3)
    for lo, hi in chunks:
        scores = dot(qs[lo:hi, :], ks[:hi, :], ((1,), (1,)))
        weights = (scores * decay_s[lo:hi, :hi]).astype(BF16)
        attn_s[lo:hi, :] = dot(weights, vs[:hi, :])
    gcol[...] = reach

    enter[...] = jnp.zeros_like(enter)
    factor[...] = jnp.ones_like(factor)
    for d in range(1, nchip):
        @pl.when(chip >= d)
        def _():
            to_chip(d).wait_recv()
            state, held = get_message(chip_in.at[d - 1])
            enter[...] += factor[...] * state
            factor[...] = factor[...] * held
    state = enter[...]
    state = jnp.where(first_core, state, pair_keep * state + pair_state)
    state_hi = state.astype(BF16)
    state_low = (state - state_hi.astype(F32)).astype(BF16)

    back = []
    for d in list(range(1, nh)) + [0]:
        peer = lax.rem(head + d, nh)
        rows = quarter(peer)
        q = qs[rows, :]
        attn = attn_s[rows, :] + gcol[rows, :] * (dot(q, state_hi) + dot(q, state_low))
        meansq = jnp.mean(attn * attn, axis=1, keepdims=True)
        osend[rows, :] = (attn * lax.rsqrt(meansq + 1e-05) * gain_s[...]).astype(BF16)
        if d:
            copy = pltpu.make_async_remote_copy(
                src_ref=osend.at[rows], dst_ref=o_ref.at[:, columns(head)],
                send_sem=out_send.at[d - 1], recv_sem=out_recv.at[d - 1],
                device_id=(ctx, peer), device_id_type=mesh_id,
            )
        else:
            copy = pltpu.make_async_copy(
                osend.at[rows], o_ref.at[:, columns(head)], own_sem.at[10]
            )
        copy.start()
        back.append(copy)

    to_pair.wait_send()
    for copy in sends.values():
        copy.wait_send()
    for d in range(1, nchip):
        @pl.when(chip + d < nchip)
        def _():
            to_chip(d).wait_send()
    for copy in back:
        copy.wait()


def fused_device(queries, keys, values, log_decay, gain, doc_starts):
    nh, nctx = lax.axis_size("head"), lax.axis_size("ctx")
    nchip = nctx // 2
    hops = max(nchip - 1, 1)
    tokens, width = queries.shape
    group = tokens * nh
    decays = log_decay.T
    hbm = pl.BlockSpec(memory_space=pltpu.HBM)
    dma = pltpu.SemaphoreType.DMA
    message = (E + KEEP_ROWS, E)
    return pl.pallas_call(
        functools.partial(fused, nh, nchip),
        out_shape=jax.ShapeDtypeStruct(queries.shape, queries.dtype),
        in_specs=[hbm] * 6,
        out_specs=pl.BlockSpec(memory_space=pl.ANY),
        scratch_shapes=[
            pltpu.VMEM((tokens, width), BF16),
            pltpu.VMEM((tokens, width), BF16),
            pltpu.VMEM((tokens, width), BF16),
            pltpu.VMEM(decays.shape, BF16),
            pltpu.SMEM(doc_starts.shape, jnp.int32),
            pltpu.VMEM((group, E), BF16),
            pltpu.VMEM((group, E), BF16),
            pltpu.VMEM((group, E), BF16),
            pltpu.VMEM((nh, *decays.shape), BF16),
            pltpu.VMEM((1, E), F32),
            pltpu.VMEM((group, group), BF16),
            pltpu.VMEM((group, group), F32),
            pltpu.VMEM((group, group), F32),
            pltpu.VMEM((group, E), F32),
            pltpu.VMEM(message, BF16),
            pltpu.VMEM(message, BF16),
            pltpu.VMEM(message, BF16),
            pltpu.VMEM((hops, *message), BF16),
            pltpu.VMEM((E, E), F32),
            pltpu.VMEM((1, E), F32),
            pltpu.VMEM((group, E), F32),
            pltpu.VMEM((group, E), BF16),
            dma((11,)),
            dma((4, nh - 1)),
            dma((4, nh - 1)),
            dma((2,)),
            dma((hops,)),
            dma((hops,)),
            dma((nh - 1,)),
            dma((nh - 1,)),
        ],
        compiler_params=pltpu.CompilerParams(
            collective_id=0, has_side_effects=True, vmem_limit_bytes=67108864
        ),
        cost_estimate=pl.CostEstimate(
            flops=2 * group * E * (2 * group + 3 * E) + 2 * group**3,
            bytes_accessed=8 * group * E,
            transcendentals=group * group,
        ),
    )(queries, keys, values, decays, gain.reshape(1, E), doc_starts)


def per_device(queries, keys, values, log_decay, gain, doc_starts):
    nh, nctx = lax.axis_size("head"), lax.axis_size("ctx")
    tokens = queries.shape[0]
    one_block = tokens * nh <= block_cap and tokens % 16 == 0
    if one_block and gain.shape[0] == E and nh > 1 and nctx % 2 == 0:
        return fused_device(queries, keys, values, log_decay, gain, doc_starts)
    return scanned(queries, keys, values, log_decay, gain, doc_starts)


def solution(mesh):
    in_specs = (
        P(("ctx", "head"), None),
        P(("ctx", "head"), None),
        P(("ctx", "head"), None),
        P(("ctx", "head"), None),
        P("head"),
        P(),
    )
    out_specs = P(("ctx", "head"), None)
    return jax.shard_map(
        per_device, mesh=mesh, in_specs=in_specs, out_specs=out_specs, check_vma=False
    )
```

```python
import functools

import jax
import jax.numpy as jnp
from jax import lax
from jax.experimental import pallas as pl
from jax.experimental.pallas import tpu as pltpu
from jax.sharding import PartitionSpec as P

E = 128


block_cap = 512


def carried_in(value, axis, join, neutral):
    count, mine = (lax.axis_size(axis), lax.axis_index(axis))
    pieces = jax.tree.map(lambda part: lax.all_gather(part, axis), value)
    total = jax.tree.map(
        lambda part, zero: jnp.full_like(part, 0) + jnp.asarray(zero, part.dtype), value, neutral
    )

    def hop(position, total):
        longer = join(total, jax.tree.map(lambda part: part[position], pieces))
        return jax.tree.map(lambda new, old: jnp.where(position < mine, new, old), longer, total)

    return lax.fori_loop(0, count - 1, hop, total)


def combine(earlier, later):
    return (earlier[0] * later[0], later[0][:, None, None] * earlier[1] + later[1])


def scanned(queries, keys, values, log_decay, gain, doc_starts):
    heads = gain.shape[0] // E
    q_group = lax.all_to_all(queries, "head", split_axis=1, concat_axis=0, tiled=True)
    k_group, v_group, g_group = (
        lax.all_to_all(keys, "head", split_axis=1, concat_axis=0, tiled=True),
        lax.all_to_all(values, "head", split_axis=1, concat_axis=0, tiled=True),
        lax.all_to_all(log_decay, "head", split_axis=1, concat_axis=0, tiled=True),
    )
    group = q_group.shape[0]
    block = min(block_cap, group)
    nblk = group // block
    ndoc = doc_starts.shape[0] - 1
    offset = lax.axis_index("ctx") * group
    token_positions = offset + jnp.arange(group, dtype=jnp.int32)
    doc_id = jnp.sum(
        (token_positions[:, None] >= doc_starts[None, 1:ndoc]).astype(jnp.int32), axis=1
    )
    is_start = jnp.any(token_positions[:, None] == doc_starts[None, 0:ndoc], axis=1)
    qb = q_group.reshape(nblk, block, heads, E)
    kb = k_group.reshape(nblk, block, heads, E)
    vb = v_group.reshape(nblk, block, heads, E)
    gb = g_group.reshape(nblk, block, heads)
    docb = doc_id.reshape(nblk, block)
    startb = is_start.reshape(nblk, block)
    rows = jnp.arange(block, dtype=jnp.int32)

    def local_block(carry, item):
        acc_a, acc_s = carry
        qx, kx, vx, gx, dx, sx = item
        cum = jnp.cumsum(gx.astype(jnp.float32), axis=0)
        opened = jnp.cumsum(sx.astype(jnp.int32)) == 0
        mask = (rows[None, :] <= rows[:, None]) & (dx[:, None] == dx[None, :])
        cum_t = cum.T
        diff = cum_t[:, :, None] - cum_t[:, None, :]
        decay = jnp.where(mask[None], jnp.exp(jnp.where(mask[None], diff, 0.0)), 0.0)
        scores = jnp.einsum("thd,jhd->htj", qx, kx, preferred_element_type=jnp.float32)
        weights = (scores * decay).astype(jnp.bfloat16)
        intra = jnp.einsum("htj,jhe->the", weights, vx, preferred_element_type=jnp.float32)
        last = cum[-1]
        tail = jnp.exp(last[None, :] - cum) * (dx == dx[-1])[:, None].astype(jnp.float32)
        scaled_keys = (kx.astype(jnp.float32) * tail[:, :, None]).astype(jnp.bfloat16)
        summary = jnp.einsum("jhe,jhf->hef", scaled_keys, vx, preferred_element_type=jnp.float32)
        keep = jnp.exp(last) * opened[-1].astype(jnp.float32)
        reach = jnp.exp(cum) * opened[:, None].astype(jnp.float32)
        updated = (acc_a * keep, keep[:, None, None] * acc_s + summary)
        return (updated, (intra, reach, acc_a, acc_s))

    start_carry = (jnp.ones((heads,), jnp.float32), jnp.zeros((heads, E, E), jnp.float32))
    device_sum, stacked = lax.scan(local_block, start_carry, (qb, kb, vb, gb, docb, startb))
    intra, reach, pre_a, pre_s = stacked
    dev_a, dev_s = device_sum
    enter_a, enter_s = carried_in((dev_a, dev_s), "ctx", combine, start_carry)
    block_in = pre_a[:, :, None, None] * enter_s[None] + pre_s
    scaled_q = qb.astype(jnp.float32) * reach[..., None]
    inter = jnp.einsum("bthe,bhef->bthf", scaled_q, block_in, precision=lax.Precision.HIGHEST)
    attn = intra + inter
    meansq = jnp.mean(attn * attn, axis=-1, keepdims=True)
    normed = attn * lax.rsqrt(meansq + 1e-05) * gain.reshape(heads, E)[None, None]
    result = normed.astype(jnp.bfloat16).reshape(group, heads * E)
    return lax.all_to_all(result, "head", split_axis=0, concat_axis=1, tiled=True)


KEEP_ROWS = 16
F32, BF16 = jnp.float32, jnp.bfloat16


def dot(a, b, dims=((1,), (0,))):
    return lax.dot_general(a, b, (dims, ((), ())), preferred_element_type=F32)


def split3(x):
    hi = x.astype(BF16).astype(F32)
    mid = (x - hi).astype(BF16).astype(F32)
    return hi, mid, x - hi - mid


def put_message(ref, state, keep):
    hi, mid, low = split3(jnp.broadcast_to(keep, (KEEP_ROWS, E)))
    row = lax.broadcasted_iota(jnp.int32, (KEEP_ROWS, E), 0)
    zero = jnp.zeros_like(hi)
    rows = jnp.where(row == 0, hi, jnp.where(row == 1, mid, jnp.where(row == 2, low, zero)))
    ref[pl.ds(0, E), :] = state.astype(BF16)
    ref[pl.ds(E, KEEP_ROWS), :] = rows.astype(BF16)


def get_message(ref):
    state = ref[pl.ds(0, E), :].astype(F32)
    keep = jnp.sum(ref[pl.ds(E, KEEP_ROWS), :].astype(F32), axis=0, keepdims=True)
    return state, keep


def fused(
    nh, nchip, q_ref, k_ref, v_ref, g_ref, gain_ref, ds_hbm, o_ref,
    ql, kl, vl, gl, ds_ref, qs, ks, vs, gs, gain_s, lower_s, later_s, decay_s, gcol,
    mine_m, pair_m, chip_m, chip_in, enter, factor, attn_s, osend,
    own_sem, send_sem, recv_sem, pair_sem, chip_send, chip_recv, out_send, out_recv,
):
    ctx, head = lax.axis_index("ctx"), lax.axis_index("head")
    tokens = k_ref.shape[0]
    group = tokens * nh
    chunk = E if group % E == 0 else group
    chunks = [(i * chunk, (i + 1) * chunk) for i in range(group // chunk)]
    chip, core = ctx // 2, ctx % 2
    sibling = ctx + 1 - 2 * core
    mesh_id = pl.DeviceIdType.MESH

    def columns(h):
        return pl.ds(pl.multiple_of(h * E, E), E)

    def quarter(h):
        return pl.ds(pl.multiple_of(h * tokens, tokens), tokens)

    local = (gl, kl, vl, ql)
    loads = [
        pltpu.make_async_copy(ref, buf, own_sem.at[a])
        for a, (ref, buf) in enumerate(zip((g_ref, k_ref, v_ref, q_ref), local))
    ]
    loads.append(pltpu.make_async_copy(gain_ref, gain_s, own_sem.at[4]))
    loads.append(pltpu.make_async_copy(ds_hbm, ds_ref, own_sem.at[5]))
    for copy in loads:
        copy.start()

    barrier = pltpu.get_barrier_semaphore()
    partners = [(ctx, lax.rem(head + d, nh)) for d in range(1, nh)] + [(sibling, head)]
    partners += [(lax.rem(chip + d, nchip) * 2 + core, head) for d in range(1, nchip)]
    for partner in partners:
        pl.semaphore_signal(barrier, inc=1, device_id=partner, device_id_type=mesh_id)

    t_wide = lax.broadcasted_iota(jnp.int32, (group, group), 0)
    j_wide = lax.broadcasted_iota(jnp.int32, (group, group), 1)
    lower_s[...] = jnp.where(t_wide >= j_wide, 1.0, 0.0).astype(BF16)
    later_s[...] = jnp.where(t_wide > j_wide, 1.0, 0.0)

    for a in range(4):
        loads[a].wait()
    pl.semaphore_wait(barrier, len(partners))

    places = (gs, ks, vs, qs)

    def piece(a, h):
        return gl if a == 0 else local[a].at[:, columns(h)]

    def place(a, h):
        return gs.at[h] if a == 0 else places[a].at[quarter(h)]

    sends = {}
    for a in range(4):
        for d in range(1, nh):
            peer = lax.rem(head + d, nh)
            sends[a, d] = pltpu.make_async_remote_copy(
                src_ref=piece(a, peer), dst_ref=place(a, head),
                send_sem=send_sem.at[a, d - 1], recv_sem=recv_sem.at[a, d - 1],
                device_id=(ctx, peer), device_id_type=mesh_id,
            )
            sends[a, d].start()
    own = [
        pltpu.make_async_copy(piece(a, head), place(a, head), own_sem.at[6 + a])
        for a in range(4)
    ]
    for copy in own:
        copy.start()

    def arrived(a):
        own[a].wait()
        for d in range(1, nh):
            sends[a, d].wait_recv()

    loads[4].wait()
    loads[5].wait()
    offset = ctx * group
    ndoc = ds_ref.shape[0] - 1
    last_token = offset + group - 1
    t_pos = offset + lax.broadcasted_iota(jnp.int32, (group, E), 0)
    begun = jnp.zeros((group, E), jnp.int32)
    begun_last = jnp.int32(0)
    for m in range(ndoc):
        s = ds_ref[m]
        begun = jnp.where(t_pos >= s, s, begun)
        begun_last = jnp.where(last_token >= s, s, begun_last)

    arrived(0)
    ones = jnp.ones((gs.shape[1], E), BF16)
    row = lax.broadcasted_iota(jnp.int32, gs.shape[1:], 0)
    for t in range(nh):
        rows = jnp.where(row == head, gs[t].astype(F32), 0.0).astype(BF16)
        gcol[pl.ds(t * tokens, tokens), :] = dot(rows, ones, ((0,), (0,)))
    g_lanes = gcol[...]
    cum = dot(lower_s[...], g_lanes.astype(BF16))
    reach = jnp.exp(cum) * jnp.where(begun < offset, 1.0, 0.0)
    tail = jnp.exp(cum[group - 1 :, :] - cum) * jnp.where(t_pos >= begun_last, 1.0, 0.0)
    keep = reach[group - 1 :, :]
    for lo, hi in chunks:
        steps = (later_s[:hi, :hi] * g_lanes[:hi, :1]).astype(BF16)
        between = dot(lower_s[lo:hi, :hi], steps)
        t_at = lo + lax.broadcasted_iota(jnp.int32, (hi - lo, hi), 0)
        j_at = lax.broadcasted_iota(jnp.int32, (hi - lo, hi), 1)
        allowed = (j_at <= t_at) & (j_at + offset >= begun[lo:hi, :1])
        decay_s[lo:hi, :hi] = jnp.where(allowed, jnp.exp(between), 0.0)

    arrived(1)
    scaled = (ks[...].astype(F32) * tail).astype(BF16)
    arrived(2)
    summary = dot(scaled, vs[...], ((0,), (0,)))
    put_message(mine_m, summary, keep)
    to_pair = pltpu.make_async_remote_copy(
        src_ref=mine_m, dst_ref=pair_m, send_sem=pair_sem.at[0], recv_sem=pair_sem.at[1],
        device_id=(sibling, head), device_id_type=mesh_id,
    )
    to_pair.start()

    to_pair.wait_recv()
    pair_state, pair_keep = get_message(pair_m)
    first_core = core == 0
    total = jnp.where(
        first_core, pair_keep * summary + pair_state, keep * pair_state + summary
    )
    put_message(chip_m, total, pair_keep * keep)

    def to_chip(d):
        return pltpu.make_async_remote_copy(
            src_ref=chip_m, dst_ref=chip_in.at[d - 1],
            send_sem=chip_send.at[d - 1], recv_sem=chip_recv.at[d - 1],
            device_id=(lax.rem(chip + d, nchip) * 2 + core, head), device_id_type=mesh_id,
        )

    for d in range(1, nchip):
        @pl.when(chip + d < nchip)
        def _():
            to_chip(d).start()

    arrived(3)
    for lo, hi in chunks:
        scores = dot(qs[lo:hi, :], ks[:hi, :], ((1,), (1,)))
        weights = (scores * decay_s[lo:hi, :hi]).astype(BF16)
        attn_s[lo:hi, :] = dot(weights, vs[:hi, :])
    gcol[...] = reach

    enter[...] = jnp.zeros_like(enter)
    factor[...] = jnp.ones_like(factor)
    for d in range(1, nchip):
        @pl.when(chip >= d)
        def _():
            to_chip(d).wait_recv()
            state, held = get_message(chip_in.at[d - 1])
            enter[...] += factor[...] * state
            factor[...] = factor[...] * held
    state = enter[...]
    state = jnp.where(first_core, state, pair_keep * state + pair_state)
    state_hi = state.astype(BF16)
    state_low = (state - state_hi.astype(F32)).astype(BF16)

    back = []
    for d in list(range(1, nh)) + [0]:
        peer = lax.rem(head + d, nh)
        rows = quarter(peer)
        q = qs[rows, :]
        attn = attn_s[rows, :] + gcol[rows, :] * (dot(q, state_hi) + dot(q, state_low))
        meansq = jnp.mean(attn * attn, axis=1, keepdims=True)
        osend[rows, :] = (attn * lax.rsqrt(meansq + 1e-05) * gain_s[...]).astype(BF16)
        if d:
            copy = pltpu.make_async_remote_copy(
                src_ref=osend.at[rows], dst_ref=o_ref.at[:, columns(head)],
                send_sem=out_send.at[d - 1], recv_sem=out_recv.at[d - 1],
                device_id=(ctx, peer), device_id_type=mesh_id,
            )
        else:
            copy = pltpu.make_async_copy(
                osend.at[rows], o_ref.at[:, columns(head)], own_sem.at[10]
            )
        copy.start()
        back.append(copy)

    to_pair.wait_send()
    for copy in sends.values():
        copy.wait_send()
    for d in range(1, nchip):
        @pl.when(chip + d < nchip)
        def _():
            to_chip(d).wait_send()
    for copy in back:
        copy.wait()


def in_hbm(x):
    return pltpu.with_memory_space_constraint(x, pltpu.HBM)


def fused_device(queries, keys, values, log_decay, gain, doc_starts):
    nh, nctx = lax.axis_size("head"), lax.axis_size("ctx")
    nchip = nctx // 2
    hops = max(nchip - 1, 1)
    tokens, width = queries.shape
    group = tokens * nh
    decays = log_decay.T
    hbm = pl.BlockSpec(memory_space=pltpu.HBM)
    dma = pltpu.SemaphoreType.DMA
    message = (E + KEEP_ROWS, E)
    return pl.pallas_call(
        functools.partial(fused, nh, nchip),
        out_shape=pltpu.VMEM(queries.shape, queries.dtype),
        in_specs=[hbm] * 6,
        out_specs=pl.BlockSpec(memory_space=pltpu.VMEM),
        scratch_shapes=[
            pltpu.VMEM((tokens, width), BF16),
            pltpu.VMEM((tokens, width), BF16),
            pltpu.VMEM((tokens, width), BF16),
            pltpu.VMEM(decays.shape, BF16),
            pltpu.SMEM(doc_starts.shape, jnp.int32),
            pltpu.VMEM((group, E), BF16),
            pltpu.VMEM((group, E), BF16),
            pltpu.VMEM((group, E), BF16),
            pltpu.VMEM((nh, *decays.shape), BF16),
            pltpu.VMEM((1, E), F32),
            pltpu.VMEM((group, group), BF16),
            pltpu.VMEM((group, group), F32),
            pltpu.VMEM((group, group), F32),
            pltpu.VMEM((group, E), F32),
            pltpu.VMEM(message, BF16),
            pltpu.VMEM(message, BF16),
            pltpu.VMEM(message, BF16),
            pltpu.VMEM((hops, *message), BF16),
            pltpu.VMEM((E, E), F32),
            pltpu.VMEM((1, E), F32),
            pltpu.VMEM((group, E), F32),
            pltpu.VMEM((group, E), BF16),
            dma((11,)),
            dma((4, nh - 1)),
            dma((4, nh - 1)),
            dma((2,)),
            dma((hops,)),
            dma((hops,)),
            dma((nh - 1,)),
            dma((nh - 1,)),
        ],
        compiler_params=pltpu.CompilerParams(
            collective_id=0, has_side_effects=True, vmem_limit_bytes=32 * 1024 * 1024
        ),
        cost_estimate=pl.CostEstimate(
            flops=2 * group * E * (2 * group + 3 * E) + 2 * group**3,
            bytes_accessed=8 * group * E,
            transcendentals=group * group,
        ),
    )(*map(in_hbm, (queries, keys, values, decays, gain.reshape(1, E), doc_starts)))


def per_device(queries, keys, values, log_decay, gain, doc_starts):
    nh, nctx = lax.axis_size("head"), lax.axis_size("ctx")
    tokens = queries.shape[0]
    one_block = tokens * nh <= block_cap and tokens % 16 == 0
    if one_block and gain.shape[0] == E and nh > 1 and nctx % 2 == 0:
        return fused_device(queries, keys, values, log_decay, gain, doc_starts)
    return scanned(queries, keys, values, log_decay, gain, doc_starts)


def solution(mesh):
    in_specs = (
        P(("ctx", "head"), None),
        P(("ctx", "head"), None),
        P(("ctx", "head"), None),
        P(("ctx", "head"), None),
        P("head"),
        P(),
    )
    out_specs = P(("ctx", "head"), None)
    return jax.shard_map(
        per_device, mesh=mesh, in_specs=in_specs, out_specs=out_specs, check_vma=False
    )
```

```python
import functools

import jax
import jax.numpy as jnp
from jax import lax
from jax.experimental import pallas as pl
from jax.experimental.pallas import tpu as pltpu
from jax.sharding import PartitionSpec as P

E = 128


block_cap = 512


def carried_in(value, axis, join, neutral):
    count, mine = (lax.axis_size(axis), lax.axis_index(axis))
    pieces = jax.tree.map(lambda part: lax.all_gather(part, axis), value)
    total = jax.tree.map(
        lambda part, zero: jnp.full_like(part, 0) + jnp.asarray(zero, part.dtype), value, neutral
    )

    def hop(position, total):
        longer = join(total, jax.tree.map(lambda part: part[position], pieces))
        return jax.tree.map(lambda new, old: jnp.where(position < mine, new, old), longer, total)

    return lax.fori_loop(0, count - 1, hop, total)


def combine(earlier, later):
    return (earlier[0] * later[0], later[0][:, None, None] * earlier[1] + later[1])


def scanned(queries, keys, values, log_decay, gain, doc_starts):
    heads = gain.shape[0] // E
    q_group = lax.all_to_all(queries, "head", split_axis=1, concat_axis=0, tiled=True)
    k_group, v_group, g_group = (
        lax.all_to_all(keys, "head", split_axis=1, concat_axis=0, tiled=True),
        lax.all_to_all(values, "head", split_axis=1, concat_axis=0, tiled=True),
        lax.all_to_all(log_decay, "head", split_axis=1, concat_axis=0, tiled=True),
    )
    group = q_group.shape[0]
    block = min(block_cap, group)
    nblk = group // block
    ndoc = doc_starts.shape[0] - 1
    offset = lax.axis_index("ctx") * group
    token_positions = offset + jnp.arange(group, dtype=jnp.int32)
    doc_id = jnp.sum(
        (token_positions[:, None] >= doc_starts[None, 1:ndoc]).astype(jnp.int32), axis=1
    )
    is_start = jnp.any(token_positions[:, None] == doc_starts[None, 0:ndoc], axis=1)
    qb = q_group.reshape(nblk, block, heads, E)
    kb = k_group.reshape(nblk, block, heads, E)
    vb = v_group.reshape(nblk, block, heads, E)
    gb = g_group.reshape(nblk, block, heads)
    docb = doc_id.reshape(nblk, block)
    startb = is_start.reshape(nblk, block)
    rows = jnp.arange(block, dtype=jnp.int32)

    def local_block(carry, item):
        acc_a, acc_s = carry
        qx, kx, vx, gx, dx, sx = item
        cum = jnp.cumsum(gx.astype(jnp.float32), axis=0)
        opened = jnp.cumsum(sx.astype(jnp.int32)) == 0
        mask = (rows[None, :] <= rows[:, None]) & (dx[:, None] == dx[None, :])
        cum_t = cum.T
        diff = cum_t[:, :, None] - cum_t[:, None, :]
        decay = jnp.where(mask[None], jnp.exp(jnp.where(mask[None], diff, 0.0)), 0.0)
        scores = jnp.einsum("thd,jhd->htj", qx, kx, preferred_element_type=jnp.float32)
        weights = (scores * decay).astype(jnp.bfloat16)
        intra = jnp.einsum("htj,jhe->the", weights, vx, preferred_element_type=jnp.float32)
        last = cum[-1]
        tail = jnp.exp(last[None, :] - cum) * (dx == dx[-1])[:, None].astype(jnp.float32)
        scaled_keys = (kx.astype(jnp.float32) * tail[:, :, None]).astype(jnp.bfloat16)
        summary = jnp.einsum("jhe,jhf->hef", scaled_keys, vx, preferred_element_type=jnp.float32)
        keep = jnp.exp(last) * opened[-1].astype(jnp.float32)
        reach = jnp.exp(cum) * opened[:, None].astype(jnp.float32)
        updated = (acc_a * keep, keep[:, None, None] * acc_s + summary)
        return (updated, (intra, reach, acc_a, acc_s))

    start_carry = (jnp.ones((heads,), jnp.float32), jnp.zeros((heads, E, E), jnp.float32))
    device_sum, stacked = lax.scan(local_block, start_carry, (qb, kb, vb, gb, docb, startb))
    intra, reach, pre_a, pre_s = stacked
    dev_a, dev_s = device_sum
    enter_a, enter_s = carried_in((dev_a, dev_s), "ctx", combine, start_carry)
    block_in = pre_a[:, :, None, None] * enter_s[None] + pre_s
    scaled_q = qb.astype(jnp.float32) * reach[..., None]
    inter = jnp.einsum("bthe,bhef->bthf", scaled_q, block_in, precision=lax.Precision.HIGHEST)
    attn = intra + inter
    meansq = jnp.mean(attn * attn, axis=-1, keepdims=True)
    normed = attn * lax.rsqrt(meansq + 1e-05) * gain.reshape(heads, E)[None, None]
    result = normed.astype(jnp.bfloat16).reshape(group, heads * E)
    return lax.all_to_all(result, "head", split_axis=0, concat_axis=1, tiled=True)


KEEP_ROWS = 16
CLOSED = -1e30
F32, BF16 = jnp.float32, jnp.bfloat16


def dot(a, b, dims=((1,), (0,))):
    return lax.dot_general(a, b, (dims, ((), ())), preferred_element_type=F32)


def split3(x):
    hi = x.astype(BF16).astype(F32)
    mid = (x - hi).astype(BF16).astype(F32)
    return hi, mid, x - hi - mid


def put_message(ref, state, keep):
    hi, mid, low = split3(jnp.broadcast_to(keep, (KEEP_ROWS, E)))
    row = lax.broadcasted_iota(jnp.int32, (KEEP_ROWS, E), 0)
    zero = jnp.zeros_like(hi)
    rows = jnp.where(row == 0, hi, jnp.where(row == 1, mid, jnp.where(row == 2, low, zero)))
    ref[pl.ds(0, E), :] = state.astype(BF16)
    ref[pl.ds(E, KEEP_ROWS), :] = rows.astype(BF16)


def get_message(ref):
    state = ref[pl.ds(0, E), :].astype(F32)
    keep = jnp.sum(ref[pl.ds(E, KEEP_ROWS), :].astype(F32), axis=0, keepdims=True)
    return state, keep


def fused(
    nh, nchip, q_ref, k_ref, v_ref, g_ref, gain_ref, ds_hbm, o_ref,
    ql, kvl, gl, ds_ref, qs, kvs, gs, gain_s, gcol,
    mine_m, pair_m, chip_m, chip_in, enter, factor, attn_s, osend,
    own_sem, send_sem, recv_sem, pair_sem, chip_send, chip_recv, out_send, out_recv,
):
    ctx, head = lax.axis_index("ctx"), lax.axis_index("head")
    tokens = k_ref.shape[0]
    group = tokens * nh
    nchunk = group // E
    kl, vl, ks, vs = kvl.at[0], kvl.at[1], kvs.at[0], kvs.at[1]
    chip, core = ctx // 2, ctx % 2
    sibling = ctx + 1 - 2 * core
    mesh_id = pl.DeviceIdType.MESH

    def columns(h):
        return pl.ds(pl.multiple_of(h * E, E), E)

    def quarter(h):
        return pl.ds(pl.multiple_of(h * tokens, tokens), tokens)

    loads = [
        pltpu.make_async_copy(ref, buf, own_sem.at[a])
        for a, (ref, buf) in enumerate(
            ((g_ref, gl), (k_ref, kl), (v_ref, vl), (q_ref, ql))
        )
    ]
    loads.append(pltpu.make_async_copy(gain_ref, gain_s, own_sem.at[4]))
    loads.append(pltpu.make_async_copy(ds_hbm, ds_ref, own_sem.at[5]))
    for copy in loads:
        copy.start()

    barrier = pltpu.get_barrier_semaphore()
    partners = [(ctx, lax.rem(head + d, nh)) for d in range(1, nh)] + [(sibling, head)]
    partners += [(lax.rem(chip + d, nchip) * 2 + core, head) for d in range(1, nchip)]
    for partner in partners:
        pl.semaphore_signal(barrier, inc=1, device_id=partner, device_id_type=mesh_id)

    t_at = lax.broadcasted_iota(jnp.int32, (E, E), 0)
    j_at = lax.broadcasted_iota(jnp.int32, (E, E), 1)
    lower = jnp.where(t_at >= j_at, 1.0, 0.0).astype(BF16)
    upper = jnp.where(t_at < j_at, 1.0, 0.0).astype(BF16)
    both = jnp.concatenate([lower, upper], axis=0)
    lower_all = jnp.concatenate([lower, jnp.ones((16, E), BF16)], axis=0)

    for a in range(4):
        loads[a].wait()
    pl.semaphore_wait(barrier, len(partners))

    def piece(a, h):
        return (gl, kvl.at[:, :, columns(h)], ql.at[:, columns(h)])[a]

    def place(a, h):
        return (gs.at[h], kvs.at[:, quarter(h), :], qs.at[quarter(h), :])[a]

    sends = {}
    for a in range(3):
        for d in range(1, nh):
            peer = lax.rem(head + d, nh)
            sends[a, d] = pltpu.make_async_remote_copy(
                src_ref=piece(a, peer), dst_ref=place(a, head),
                send_sem=send_sem.at[a, d - 1], recv_sem=recv_sem.at[a, d - 1],
                device_id=(ctx, peer), device_id_type=mesh_id,
            )
            sends[a, d].start()
    own = [
        pltpu.make_async_copy(piece(a, head), place(a, head), own_sem.at[6 + a])
        for a in range(3)
    ]
    for copy in own:
        copy.start()

    def arrived(a):
        own[a].wait()
        for d in range(1, nh):
            sends[a, d].wait_recv()

    loads[4].wait()
    loads[5].wait()
    ndoc = ds_ref.shape[0] - 1

    arrived(0)
    ones = jnp.ones((gs.shape[1], E), BF16)
    row = lax.broadcasted_iota(jnp.int32, gs.shape[1:], 0)
    at = ctx * group + lax.broadcasted_iota(jnp.int32, gs.shape[1:], 1)
    for t in range(nh):
        starts = at + t * tokens == ds_ref[0]
        for m in range(1, ndoc):
            starts = starts | (at + t * tokens == ds_ref[m])
        g = jnp.where(starts, CLOSED, gs[t].astype(F32))
        rows = jnp.where(row == head, g, 0.0).astype(BF16)
        gcol[pl.ds(t * tokens, tokens), :] = dot(rows, ones, ((0,), (0,)))

    upto, after, whole = [], [], []
    for r in range(nchunk):
        sums = dot(both, gcol[r * E : (r + 1) * E, :].astype(BF16))
        upto.append(sums[:E])
        after.append(sums[E:])
        whole.append(sums[E - 1 : E])

    def span(lo, hi):
        return sum(whole[lo:hi], jnp.zeros((1, E), F32))

    keep = jnp.exp(span(0, nchunk))

    arrived(1)
    summary = jnp.zeros((E, E), F32)
    for r in range(nchunk):
        rows = slice(r * E, (r + 1) * E)
        tail = jnp.exp(after[r] + span(r + 1, nchunk))
        scaled = (ks[rows, :].astype(F32) * tail).astype(BF16)
        summary += dot(scaled, vs[rows, :], ((0,), (0,)))
    put_message(mine_m, summary, keep)
    to_pair = pltpu.make_async_remote_copy(
        src_ref=mine_m, dst_ref=pair_m, send_sem=pair_sem.at[0], recv_sem=pair_sem.at[1],
        device_id=(sibling, head), device_id_type=mesh_id,
    )
    to_pair.start()

    within, rest, reached = [], [], []
    for r in range(nchunk):
        steps = jnp.where(t_at > j_at, gcol[r * E : (r + 1) * E, :], 0.0).astype(BF16)
        between = dot(lower_all, steps)
        within.append(jnp.where(t_at >= j_at, jnp.exp(between[:E]), 0.0))
        rest.append(between[E : E + 1])
        reached.append(jnp.exp(upto[r]))

    to_pair.wait_recv()
    pair_state, pair_keep = get_message(pair_m)
    first_core = core == 0
    total = jnp.where(
        first_core, pair_keep * summary + pair_state, keep * pair_state + summary
    )
    put_message(chip_m, total, pair_keep * keep)

    def to_chip(d):
        return pltpu.make_async_remote_copy(
            src_ref=chip_m, dst_ref=chip_in.at[d - 1],
            send_sem=chip_send.at[d - 1], recv_sem=chip_recv.at[d - 1],
            device_id=(lax.rem(chip + d, nchip) * 2 + core, head), device_id_type=mesh_id,
        )

    for d in range(1, nchip):
        @pl.when(chip + d < nchip)
        def _():
            to_chip(d).start()

    arrived(2)
    for r in range(nchunk):
        rows = slice(r * E, (r + 1) * E)
        scores = dot(qs[rows, :], ks[: (r + 1) * E, :], ((1,), (1,)))
        weights = []
        for c in range(r):
            decay = reached[r] * jnp.exp(rest[c] + span(c + 1, r))
            weights.append((scores[:, c * E : (c + 1) * E] * decay).astype(BF16))
        weights.append((scores[:, r * E :] * within[r]).astype(BF16))
        weights = jnp.concatenate(weights, axis=1)
        attn_s[rows, :] = dot(weights, vs[: (r + 1) * E, :])
        gcol[rows, :] = reached[r] * jnp.exp(span(0, r))

    enter[...] = jnp.zeros_like(enter)
    factor[...] = jnp.ones_like(factor)
    for d in range(1, nchip):
        @pl.when(chip >= d)
        def _():
            to_chip(d).wait_recv()
            state, held = get_message(chip_in.at[d - 1])
            enter[...] += factor[...] * state
            factor[...] = factor[...] * held
    state = enter[...]
    state = jnp.where(first_core, state, pair_keep * state + pair_state)
    state_hi = state.astype(BF16)
    state_low = (state - state_hi.astype(F32)).astype(BF16)

    back = []
    for d in list(range(1, nh)) + [0]:
        peer = lax.rem(head + d, nh)
        rows = quarter(peer)
        q = qs[rows, :]
        attn = attn_s[rows, :] + gcol[rows, :] * (dot(q, state_hi) + dot(q, state_low))
        meansq = jnp.mean(attn * attn, axis=1, keepdims=True)
        osend[rows, :] = (attn * lax.rsqrt(meansq + 1e-05) * gain_s[...]).astype(BF16)
        if d:
            copy = pltpu.make_async_remote_copy(
                src_ref=osend.at[rows], dst_ref=o_ref.at[:, columns(head)],
                send_sem=out_send.at[d - 1], recv_sem=out_recv.at[d - 1],
                device_id=(ctx, peer), device_id_type=mesh_id,
            )
        else:
            copy = pltpu.make_async_copy(
                osend.at[rows], o_ref.at[:, columns(head)], own_sem.at[9]
            )
        copy.start()
        back.append(copy)

    to_pair.wait_send()
    for copy in sends.values():
        copy.wait_send()
    for d in range(1, nchip):
        @pl.when(chip + d < nchip)
        def _():
            to_chip(d).wait_send()
    for copy in back:
        copy.wait()


def in_hbm(x):
    return pltpu.with_memory_space_constraint(x, pltpu.HBM)


def fused_device(queries, keys, values, log_decay, gain, doc_starts):
    nh, nctx = lax.axis_size("head"), lax.axis_size("ctx")
    nchip = nctx // 2
    hops = max(nchip - 1, 1)
    tokens, width = queries.shape
    group = tokens * nh
    decays = log_decay.T
    hbm = pl.BlockSpec(memory_space=pltpu.HBM)
    dma = pltpu.SemaphoreType.DMA
    message = (E + KEEP_ROWS, E)
    return pl.pallas_call(
        functools.partial(fused, nh, nchip),
        out_shape=pltpu.VMEM(queries.shape, queries.dtype),
        in_specs=[hbm] * 6,
        out_specs=pl.BlockSpec(memory_space=pltpu.VMEM),
        scratch_shapes=[
            pltpu.VMEM((tokens, width), BF16),
            pltpu.VMEM((2, tokens, width), BF16),
            pltpu.VMEM(decays.shape, BF16),
            pltpu.SMEM(doc_starts.shape, jnp.int32),
            pltpu.VMEM((group, E), BF16),
            pltpu.VMEM((2, group, E), BF16),
            pltpu.VMEM((nh, *decays.shape), BF16),
            pltpu.VMEM((1, E), F32),
            pltpu.VMEM((group, E), F32),
            pltpu.VMEM(message, BF16),
            pltpu.VMEM(message, BF16),
            pltpu.VMEM(message, BF16),
            pltpu.VMEM((hops, *message), BF16),
            pltpu.VMEM((E, E), F32),
            pltpu.VMEM((1, E), F32),
            pltpu.VMEM((group, E), F32),
            pltpu.VMEM((group, E), BF16),
            dma((10,)),
            dma((3, nh - 1)),
            dma((3, nh - 1)),
            dma((2,)),
            dma((hops,)),
            dma((hops,)),
            dma((nh - 1,)),
            dma((nh - 1,)),
        ],
        compiler_params=pltpu.CompilerParams(
            collective_id=0, has_side_effects=True, vmem_limit_bytes=32 * 1024 * 1024
        ),
        cost_estimate=pl.CostEstimate(
            flops=2 * group * E * (2 * group + 3 * E) + 2 * group**3,
            bytes_accessed=8 * group * E,
            transcendentals=group * group,
        ),
    )(*map(in_hbm, (queries, keys, values, decays, gain.reshape(1, E), doc_starts)))


def per_device(queries, keys, values, log_decay, gain, doc_starts):
    nh, nctx = lax.axis_size("head"), lax.axis_size("ctx")
    tokens = queries.shape[0]
    one_block = tokens * nh <= block_cap and tokens % 16 == 0 and tokens * nh % E == 0
    if one_block and gain.shape[0] == E and nh > 1 and nctx % 2 == 0:
        return fused_device(queries, keys, values, log_decay, gain, doc_starts)
    return scanned(queries, keys, values, log_decay, gain, doc_starts)


def solution(mesh):
    in_specs = (
        P(("ctx", "head"), None),
        P(("ctx", "head"), None),
        P(("ctx", "head"), None),
        P(("ctx", "head"), None),
        P("head"),
        P(),
    )
    out_specs = P(("ctx", "head"), None)
    return jax.shard_map(
        per_device, mesh=mesh, in_specs=in_specs, out_specs=out_specs, check_vma=False
    )
```

```python
import functools

import jax
import jax.numpy as jnp
from jax import lax
from jax.experimental import pallas as pl
from jax.experimental.pallas import tpu as pltpu
from jax.sharding import PartitionSpec as P

E = 128


block_cap = 512


def carried_in(value, axis, join, neutral):
    count, mine = (lax.axis_size(axis), lax.axis_index(axis))
    pieces = jax.tree.map(lambda part: lax.all_gather(part, axis), value)
    total = jax.tree.map(
        lambda part, zero: jnp.full_like(part, 0) + jnp.asarray(zero, part.dtype), value, neutral
    )

    def hop(position, total):
        longer = join(total, jax.tree.map(lambda part: part[position], pieces))
        return jax.tree.map(lambda new, old: jnp.where(position < mine, new, old), longer, total)

    return lax.fori_loop(0, count - 1, hop, total)


def combine(earlier, later):
    return (earlier[0] * later[0], later[0][:, None, None] * earlier[1] + later[1])


def scanned(queries, keys, values, log_decay, gain, doc_starts):
    heads = gain.shape[0] // E
    q_group = lax.all_to_all(queries, "head", split_axis=1, concat_axis=0, tiled=True)
    k_group, v_group, g_group = (
        lax.all_to_all(keys, "head", split_axis=1, concat_axis=0, tiled=True),
        lax.all_to_all(values, "head", split_axis=1, concat_axis=0, tiled=True),
        lax.all_to_all(log_decay, "head", split_axis=1, concat_axis=0, tiled=True),
    )
    group = q_group.shape[0]
    block = min(block_cap, group)
    nblk = group // block
    ndoc = doc_starts.shape[0] - 1
    offset = lax.axis_index("ctx") * group
    token_positions = offset + jnp.arange(group, dtype=jnp.int32)
    doc_id = jnp.sum(
        (token_positions[:, None] >= doc_starts[None, 1:ndoc]).astype(jnp.int32), axis=1
    )
    is_start = jnp.any(token_positions[:, None] == doc_starts[None, 0:ndoc], axis=1)
    qb = q_group.reshape(nblk, block, heads, E)
    kb = k_group.reshape(nblk, block, heads, E)
    vb = v_group.reshape(nblk, block, heads, E)
    gb = g_group.reshape(nblk, block, heads)
    docb = doc_id.reshape(nblk, block)
    startb = is_start.reshape(nblk, block)
    rows = jnp.arange(block, dtype=jnp.int32)

    def local_block(carry, item):
        acc_a, acc_s = carry
        qx, kx, vx, gx, dx, sx = item
        cum = jnp.cumsum(gx.astype(jnp.float32), axis=0)
        opened = jnp.cumsum(sx.astype(jnp.int32)) == 0
        mask = (rows[None, :] <= rows[:, None]) & (dx[:, None] == dx[None, :])
        cum_t = cum.T
        diff = cum_t[:, :, None] - cum_t[:, None, :]
        decay = jnp.where(mask[None], jnp.exp(jnp.where(mask[None], diff, 0.0)), 0.0)
        scores = jnp.einsum("thd,jhd->htj", qx, kx, preferred_element_type=jnp.float32)
        weights = (scores * decay).astype(jnp.bfloat16)
        intra = jnp.einsum("htj,jhe->the", weights, vx, preferred_element_type=jnp.float32)
        last = cum[-1]
        tail = jnp.exp(last[None, :] - cum) * (dx == dx[-1])[:, None].astype(jnp.float32)
        scaled_keys = (kx.astype(jnp.float32) * tail[:, :, None]).astype(jnp.bfloat16)
        summary = jnp.einsum("jhe,jhf->hef", scaled_keys, vx, preferred_element_type=jnp.float32)
        keep = jnp.exp(last) * opened[-1].astype(jnp.float32)
        reach = jnp.exp(cum) * opened[:, None].astype(jnp.float32)
        updated = (acc_a * keep, keep[:, None, None] * acc_s + summary)
        return (updated, (intra, reach, acc_a, acc_s))

    start_carry = (jnp.ones((heads,), jnp.float32), jnp.zeros((heads, E, E), jnp.float32))
    device_sum, stacked = lax.scan(local_block, start_carry, (qb, kb, vb, gb, docb, startb))
    intra, reach, pre_a, pre_s = stacked
    dev_a, dev_s = device_sum
    enter_a, enter_s = carried_in((dev_a, dev_s), "ctx", combine, start_carry)
    block_in = pre_a[:, :, None, None] * enter_s[None] + pre_s
    scaled_q = qb.astype(jnp.float32) * reach[..., None]
    inter = jnp.einsum("bthe,bhef->bthf", scaled_q, block_in, precision=lax.Precision.HIGHEST)
    attn = intra + inter
    meansq = jnp.mean(attn * attn, axis=-1, keepdims=True)
    normed = attn * lax.rsqrt(meansq + 1e-05) * gain.reshape(heads, E)[None, None]
    result = normed.astype(jnp.bfloat16).reshape(group, heads * E)
    return lax.all_to_all(result, "head", split_axis=0, concat_axis=1, tiled=True)


KEEP_ROWS = 16
CLOSED = -1e30
F32, BF16 = jnp.float32, jnp.bfloat16


def dot(a, b, dims=((1,), (0,))):
    return lax.dot_general(a, b, (dims, ((), ())), preferred_element_type=F32)


def split3(x):
    hi = x.astype(BF16).astype(F32)
    mid = (x - hi).astype(BF16).astype(F32)
    return hi, mid, x - hi - mid


def put_message(ref, state, keep):
    hi, mid, low = split3(jnp.broadcast_to(keep, (KEEP_ROWS, E)))
    row = lax.broadcasted_iota(jnp.int32, (KEEP_ROWS, E), 0)
    zero = jnp.zeros_like(hi)
    rows = jnp.where(row == 0, hi, jnp.where(row == 1, mid, jnp.where(row == 2, low, zero)))
    ref[pl.ds(0, E), :] = state.astype(BF16)
    ref[pl.ds(E, KEEP_ROWS), :] = rows.astype(BF16)


def get_message(ref):
    state = ref[pl.ds(0, E), :].astype(F32)
    keep = jnp.sum(ref[pl.ds(E, KEEP_ROWS), :].astype(F32), axis=0, keepdims=True)
    return state, keep


def fused(
    nh, nchip, q_ref, k_ref, v_ref, g_ref, gain_ref, ds_hbm, o_ref,
    ql, kvl, gl, ds_ref, qs, kvs, gs, gain_s, gcol,
    part_m, part_in, chip_m, chip_in, enter, factor, first, first_held, attn_s, osend,
    own_sem, send_sem, recv_sem, part_send, part_recv, chip_send, chip_recv,
    out_send, out_recv,
):
    ctx, head = lax.axis_index("ctx"), lax.axis_index("head")
    tokens = k_ref.shape[0]
    group = tokens * nh
    nchunk = group // E
    kl, vl, ks, vs = kvl.at[0], kvl.at[1], kvs.at[0], kvs.at[1]
    chip, core = ctx // 2, ctx % 2
    sibling, gather = ctx + 1 - 2 * core, 2 * chip + 1
    mesh_id = pl.DeviceIdType.MESH

    def columns(h):
        return pl.ds(pl.multiple_of(h * E, E), E)

    def quarter(h):
        return pl.ds(pl.multiple_of(h * tokens, tokens), tokens)

    loads = [
        pltpu.make_async_copy(ref, buf, own_sem.at[a])
        for a, (ref, buf) in enumerate(
            ((g_ref, gl), (k_ref, kl), (v_ref, vl), (q_ref, ql))
        )
    ]
    loads.append(pltpu.make_async_copy(gain_ref, gain_s, own_sem.at[4]))
    loads.append(pltpu.make_async_copy(ds_hbm, ds_ref, own_sem.at[5]))
    for copy in loads:
        copy.start()
    first[...] = jnp.zeros_like(first)
    first_held[...] = jnp.ones_like(first_held)

    barrier = pltpu.get_barrier_semaphore()
    partners = [(ctx, lax.rem(head + d, nh)) for d in range(1, nh)]
    partners += [(sibling, lax.rem(head + d, nh)) for d in range(nh)]
    partners += [
        (lax.rem(chip + d, nchip) * 2 + other, head)
        for d in range(1, nchip)
        for other in range(2)
    ]
    for partner in partners:
        pl.semaphore_signal(barrier, inc=1, device_id=partner, device_id_type=mesh_id)

    t_at = lax.broadcasted_iota(jnp.int32, (E, E), 0)
    j_at = lax.broadcasted_iota(jnp.int32, (E, E), 1)
    lower = jnp.where(t_at >= j_at, 1.0, 0.0).astype(BF16)
    lower_all = jnp.concatenate([lower, jnp.ones((16, E), BF16)], axis=0)

    loads[5].wait()
    loads[0].wait()
    ndoc = ds_ref.shape[0] - 1

    def closed(g, first_token):
        at = first_token + lax.broadcasted_iota(jnp.int32, g.shape, 1)
        starts = at == ds_ref[0]
        for m in range(1, ndoc):
            starts = starts | (at == ds_ref[m])
        return jnp.where(starts, CLOSED, g.astype(F32))

    pick = lax.broadcasted_iota(jnp.int32, (nh, nh * E), 0)
    lane = lax.broadcasted_iota(jnp.int32, (nh, nh * E), 1)
    pick = jnp.where((lane >= pick * E) & (lane < pick * E + E), 1.0, 0.0).astype(BF16)
    mine = closed(gl[...], ctx * group + head * tokens).astype(BF16)
    mine = dot(mine, pick, ((0,), (0,)))
    t_own = lax.broadcasted_iota(jnp.int32, (tokens, tokens), 0)
    j_own = lax.broadcasted_iota(jnp.int32, (tokens, tokens), 1)
    own_upper = jnp.where(t_own < j_own, 1.0, 0.0).astype(BF16)
    own_after = dot(own_upper, mine.astype(BF16))
    own_tail = jnp.exp(own_after)
    own_keep = jnp.exp(own_after[:1] + mine[:1])
    loads[1].wait()
    own_scaled = (kl[...].astype(F32) * own_tail).astype(BF16)
    loads[2].wait()
    for h in range(nh):
        cols = slice(h * E, (h + 1) * E)
        share = dot(own_scaled[:, cols], vl[:, cols], ((0,), (0,)))
        put_message(part_m.at[h], share, own_keep[:, cols])

    loads[3].wait()
    pl.semaphore_wait(barrier, len(partners))

    def share(d, from_core):
        peer = lax.rem(head + d, nh)
        return pltpu.make_async_remote_copy(
            src_ref=part_m.at[peer], dst_ref=part_in.at[core * nh + head],
            send_sem=part_send.at[d], recv_sem=part_recv.at[from_core * nh + d],
            device_id=(gather, peer), device_id_type=mesh_id,
        )

    for d in range(1, nh):
        share(d, core).start()

    @pl.when(core == 0)
    def _():
        share(0, core).start()

    @pl.when(core == 1)
    def _():
        part_in[nh + head] = part_m[head]


    def piece(a, h):
        return (gl, kvl.at[:, :, columns(h)], ql.at[:, columns(h)])[a]

    def place(a, h):
        return (gs.at[h], kvs.at[:, quarter(h), :], qs.at[quarter(h), :])[a]

    sends = {}
    for a in range(3):
        for d in range(1, nh):
            peer = lax.rem(head + d, nh)
            sends[a, d] = pltpu.make_async_remote_copy(
                src_ref=piece(a, peer), dst_ref=place(a, head),
                send_sem=send_sem.at[a, d - 1], recv_sem=recv_sem.at[a, d - 1],
                device_id=(ctx, peer), device_id_type=mesh_id,
            )
            sends[a, d].start()
    own = [
        pltpu.make_async_copy(piece(a, head), place(a, head), own_sem.at[6 + a])
        for a in range(3)
    ]
    for copy in own:
        copy.start()

    def arrived(a):
        own[a].wait()
        for d in range(1, nh):
            sends[a, d].wait_recv()

    loads[4].wait()

    def to_chip(d, other):
        return pltpu.make_async_remote_copy(
            src_ref=chip_m, dst_ref=chip_in.at[d - 1],
            send_sem=chip_send.at[d - 1, other], recv_sem=chip_recv.at[d - 1],
            device_id=(lax.rem(chip + d, nchip) * 2 + other, head),
            device_id_type=mesh_id,
        )

    @pl.when(core == 1)
    def _():
        for from_core in range(2):
            for d in range(1 if from_core else 0, nh):
                share(d, from_core).wait_recv()
        state, held = get_message(part_in.at[0])
        for i in range(1, 2 * nh):
            more, kept = get_message(part_in.at[i])
            state, held = kept * state + more, held * kept
            if i == nh - 1:
                first[...] = state
                first_held[...] = held
        put_message(chip_m, state, held)
        for d in range(1, nchip):
            @pl.when(chip + d < nchip)
            def _():
                for other in range(2):
                    to_chip(d, other).start()

    arrived(0)
    ones = jnp.ones((gs.shape[1], E), BF16)
    row = lax.broadcasted_iota(jnp.int32, gs.shape[1:], 0)
    for t in range(nh):
        g = closed(gs[t], ctx * group + t * tokens)
        rows = jnp.where(row == head, g, 0.0).astype(BF16)
        gcol[pl.ds(t * tokens, tokens), :] = dot(rows, ones, ((0,), (0,)))

    upto, whole = [], []
    for r in range(nchunk):
        sums = dot(lower, gcol[r * E : (r + 1) * E, :].astype(BF16))
        upto.append(sums)
        whole.append(sums[E - 1 :])

    def span(lo, hi):
        return sum(whole[lo:hi], jnp.zeros((1, E), F32))

    within, rest, reached = [], [], []
    for r in range(nchunk):
        steps = jnp.where(t_at > j_at, gcol[r * E : (r + 1) * E, :], 0.0).astype(BF16)
        between = dot(lower_all, steps)
        within.append(jnp.where(t_at >= j_at, jnp.exp(between[:E]), 0.0))
        rest.append(between[E : E + 1])
        reached.append(jnp.exp(upto[r]))

    arrived(1)
    arrived(2)
    for r in range(nchunk):
        rows = slice(r * E, (r + 1) * E)
        scores = dot(qs[rows, :], ks[: (r + 1) * E, :], ((1,), (1,)))
        weights = []
        for c in range(r):
            decay = reached[r] * jnp.exp(rest[c] + span(c + 1, r))
            weights.append((scores[:, c * E : (c + 1) * E] * decay).astype(BF16))
        weights.append((scores[:, r * E :] * within[r]).astype(BF16))
        weights = jnp.concatenate(weights, axis=1)
        attn_s[rows, :] = dot(weights, vs[: (r + 1) * E, :])
        gcol[rows, :] = reached[r] * jnp.exp(span(0, r))

    enter[...] = jnp.zeros_like(enter)
    factor[...] = jnp.ones_like(factor)
    for d in range(1, nchip):
        @pl.when(chip >= d)
        def _():
            to_chip(d, 0).wait_recv()
            state, held = get_message(chip_in.at[d - 1])
            enter[...] += factor[...] * state
            factor[...] = factor[...] * held
    state = enter[...]
    state = first_held[...] * state + first[...]
    state_hi = state.astype(BF16)
    state_low = (state - state_hi.astype(F32)).astype(BF16)

    back = []
    for d in list(range(1, nh)) + [0]:
        peer = lax.rem(head + d, nh)
        rows = quarter(peer)
        q = qs[rows, :]
        attn = attn_s[rows, :] + gcol[rows, :] * (dot(q, state_hi) + dot(q, state_low))
        meansq = jnp.mean(attn * attn, axis=1, keepdims=True)
        osend[rows, :] = (attn * lax.rsqrt(meansq + 1e-05) * gain_s[...]).astype(BF16)
        if d:
            copy = pltpu.make_async_remote_copy(
                src_ref=osend.at[rows], dst_ref=o_ref.at[:, columns(head)],
                send_sem=out_send.at[d - 1], recv_sem=out_recv.at[d - 1],
                device_id=(ctx, peer), device_id_type=mesh_id,
            )
        else:
            copy = pltpu.make_async_copy(
                osend.at[rows], o_ref.at[:, columns(head)], own_sem.at[9]
            )
        copy.start()
        back.append(copy)

    for copy in sends.values():
        copy.wait_send()
    for d in range(1, nh):
        share(d, core).wait_send()

    @pl.when(core == 0)
    def _():
        share(0, core).wait_send()

    @pl.when(core == 1)
    def _():
        for d in range(1, nchip):
            @pl.when(chip + d < nchip)
            def _():
                for other in range(2):
                    to_chip(d, other).wait_send()

    for copy in back:
        copy.wait()


def in_hbm(x):
    return pltpu.with_memory_space_constraint(x, pltpu.HBM)


def fused_device(queries, keys, values, log_decay, gain, doc_starts):
    nh, nctx = lax.axis_size("head"), lax.axis_size("ctx")
    nchip = nctx // 2
    hops = max(nchip - 1, 1)
    tokens, width = queries.shape
    group = tokens * nh
    decays = log_decay.T
    hbm = pl.BlockSpec(memory_space=pltpu.HBM)
    dma = pltpu.SemaphoreType.DMA
    message = (E + KEEP_ROWS, E)
    return pl.pallas_call(
        functools.partial(fused, nh, nchip),
        out_shape=pltpu.VMEM(queries.shape, queries.dtype),
        in_specs=[hbm] * 6,
        out_specs=pl.BlockSpec(memory_space=pltpu.VMEM),
        scratch_shapes=[
            pltpu.VMEM((tokens, width), BF16),
            pltpu.VMEM((2, tokens, width), BF16),
            pltpu.VMEM(decays.shape, BF16),
            pltpu.SMEM(doc_starts.shape, jnp.int32),
            pltpu.VMEM((group, E), BF16),
            pltpu.VMEM((2, group, E), BF16),
            pltpu.VMEM((nh, *decays.shape), BF16),
            pltpu.VMEM((1, E), F32),
            pltpu.VMEM((group, E), F32),
            pltpu.VMEM((nh, *message), BF16),
            pltpu.VMEM((2 * nh, *message), BF16),
            pltpu.VMEM(message, BF16),
            pltpu.VMEM((hops, *message), BF16),
            pltpu.VMEM((E, E), F32),
            pltpu.VMEM((1, E), F32),
            pltpu.VMEM((E, E), F32),
            pltpu.VMEM((1, E), F32),
            pltpu.VMEM((group, E), F32),
            pltpu.VMEM((group, E), BF16),
            dma((10,)),
            dma((3, nh - 1)),
            dma((3, nh - 1)),
            dma((nh,)),
            dma((2 * nh,)),
            dma((hops, 2)),
            dma((hops,)),
            dma((nh - 1,)),
            dma((nh - 1,)),
        ],
        compiler_params=pltpu.CompilerParams(
            collective_id=0, has_side_effects=True, vmem_limit_bytes=32 * 1024 * 1024
        ),
        cost_estimate=pl.CostEstimate(
            flops=2 * group * E * (2 * group + 3 * E) + 2 * group**3,
            bytes_accessed=8 * group * E,
            transcendentals=group * group,
        ),
    )(*map(in_hbm, (queries, keys, values, decays, gain.reshape(1, E), doc_starts)))


def per_device(queries, keys, values, log_decay, gain, doc_starts):
    nh, nctx = lax.axis_size("head"), lax.axis_size("ctx")
    tokens = queries.shape[0]
    one_block = tokens * nh <= block_cap and tokens % 16 == 0 and tokens * nh % E == 0
    if one_block and gain.shape[0] == E and nh > 1 and nctx % 2 == 0:
        return fused_device(queries, keys, values, log_decay, gain, doc_starts)
    return scanned(queries, keys, values, log_decay, gain, doc_starts)


def solution(mesh):
    in_specs = (
        P(("ctx", "head"), None),
        P(("ctx", "head"), None),
        P(("ctx", "head"), None),
        P(("ctx", "head"), None),
        P("head"),
        P(),
    )
    out_specs = P(("ctx", "head"), None)
    return jax.shard_map(
        per_device, mesh=mesh, in_specs=in_specs, out_specs=out_specs, check_vma=False
    )
```

```python
import functools

import jax
import jax.numpy as jnp
from jax import lax
from jax.experimental import pallas as pl
from jax.experimental.pallas import tpu as pltpu
from jax.sharding import PartitionSpec as P

E = 128


block_cap = 512


def carried_in(value, axis, join, neutral):
    count, mine = (lax.axis_size(axis), lax.axis_index(axis))
    pieces = jax.tree.map(lambda part: lax.all_gather(part, axis), value)
    total = jax.tree.map(
        lambda part, zero: jnp.full_like(part, 0) + jnp.asarray(zero, part.dtype), value, neutral
    )

    def hop(position, total):
        longer = join(total, jax.tree.map(lambda part: part[position], pieces))
        return jax.tree.map(lambda new, old: jnp.where(position < mine, new, old), longer, total)

    return lax.fori_loop(0, count - 1, hop, total)


def combine(earlier, later):
    return (earlier[0] * later[0], later[0][:, None, None] * earlier[1] + later[1])


def scanned(queries, keys, values, log_decay, gain, doc_starts):
    heads = gain.shape[0] // E
    q_group = lax.all_to_all(queries, "head", split_axis=1, concat_axis=0, tiled=True)
    k_group, v_group, g_group = (
        lax.all_to_all(keys, "head", split_axis=1, concat_axis=0, tiled=True),
        lax.all_to_all(values, "head", split_axis=1, concat_axis=0, tiled=True),
        lax.all_to_all(log_decay, "head", split_axis=1, concat_axis=0, tiled=True),
    )
    group = q_group.shape[0]
    block = min(block_cap, group)
    nblk = group // block
    ndoc = doc_starts.shape[0] - 1
    offset = lax.axis_index("ctx") * group
    token_positions = offset + jnp.arange(group, dtype=jnp.int32)
    doc_id = jnp.sum(
        (token_positions[:, None] >= doc_starts[None, 1:ndoc]).astype(jnp.int32), axis=1
    )
    is_start = jnp.any(token_positions[:, None] == doc_starts[None, 0:ndoc], axis=1)
    qb = q_group.reshape(nblk, block, heads, E)
    kb = k_group.reshape(nblk, block, heads, E)
    vb = v_group.reshape(nblk, block, heads, E)
    gb = g_group.reshape(nblk, block, heads)
    docb = doc_id.reshape(nblk, block)
    startb = is_start.reshape(nblk, block)
    rows = jnp.arange(block, dtype=jnp.int32)

    def local_block(carry, item):
        acc_a, acc_s = carry
        qx, kx, vx, gx, dx, sx = item
        cum = jnp.cumsum(gx.astype(jnp.float32), axis=0)
        opened = jnp.cumsum(sx.astype(jnp.int32)) == 0
        mask = (rows[None, :] <= rows[:, None]) & (dx[:, None] == dx[None, :])
        cum_t = cum.T
        diff = cum_t[:, :, None] - cum_t[:, None, :]
        decay = jnp.where(mask[None], jnp.exp(jnp.where(mask[None], diff, 0.0)), 0.0)
        scores = jnp.einsum("thd,jhd->htj", qx, kx, preferred_element_type=jnp.float32)
        weights = (scores * decay).astype(jnp.bfloat16)
        intra = jnp.einsum("htj,jhe->the", weights, vx, preferred_element_type=jnp.float32)
        last = cum[-1]
        tail = jnp.exp(last[None, :] - cum) * (dx == dx[-1])[:, None].astype(jnp.float32)
        scaled_keys = (kx.astype(jnp.float32) * tail[:, :, None]).astype(jnp.bfloat16)
        summary = jnp.einsum("jhe,jhf->hef", scaled_keys, vx, preferred_element_type=jnp.float32)
        keep = jnp.exp(last) * opened[-1].astype(jnp.float32)
        reach = jnp.exp(cum) * opened[:, None].astype(jnp.float32)
        updated = (acc_a * keep, keep[:, None, None] * acc_s + summary)
        return (updated, (intra, reach, acc_a, acc_s))

    start_carry = (jnp.ones((heads,), jnp.float32), jnp.zeros((heads, E, E), jnp.float32))
    device_sum, stacked = lax.scan(local_block, start_carry, (qb, kb, vb, gb, docb, startb))
    intra, reach, pre_a, pre_s = stacked
    dev_a, dev_s = device_sum
    enter_a, enter_s = carried_in((dev_a, dev_s), "ctx", combine, start_carry)
    block_in = pre_a[:, :, None, None] * enter_s[None] + pre_s
    scaled_q = qb.astype(jnp.float32) * reach[..., None]
    inter = jnp.einsum("bthe,bhef->bthf", scaled_q, block_in, precision=lax.Precision.HIGHEST)
    attn = intra + inter
    meansq = jnp.mean(attn * attn, axis=-1, keepdims=True)
    normed = attn * lax.rsqrt(meansq + 1e-05) * gain.reshape(heads, E)[None, None]
    result = normed.astype(jnp.bfloat16).reshape(group, heads * E)
    return lax.all_to_all(result, "head", split_axis=0, concat_axis=1, tiled=True)


KEEP_ROWS = 16
F32, BF16 = jnp.float32, jnp.bfloat16


def dot(a, b, dims=((1,), (0,))):
    return lax.dot_general(a, b, (dims, ((), ())), preferred_element_type=F32)


def split3(x):
    hi = x.astype(BF16).astype(F32)
    mid = (x - hi).astype(BF16).astype(F32)
    return hi, mid, x - hi - mid


def put_message(ref, state, keep):
    hi, mid, low = split3(jnp.broadcast_to(keep, (KEEP_ROWS, E)))
    row = lax.broadcasted_iota(jnp.int32, (KEEP_ROWS, E), 0)
    zero = jnp.zeros_like(hi)
    rows = jnp.where(row == 0, hi, jnp.where(row == 1, mid, jnp.where(row == 2, low, zero)))
    ref[pl.ds(0, E), :] = state.astype(BF16)
    ref[pl.ds(E, KEEP_ROWS), :] = rows.astype(BF16)


def get_message(ref):
    state = ref[pl.ds(0, E), :].astype(F32)
    keep = jnp.sum(ref[pl.ds(E, KEEP_ROWS), :].astype(F32), axis=0, keepdims=True)
    return state, keep


def fused(
    nh, nchip, q_ref, k_ref, v_ref, g_ref, gain_ref, ds_hbm, o_ref,
    ql, kl, vl, gl, ds_ref, qs, ks, vs, gs, gain_s, lower_s, later_s, decay_s, gcol,
    mine_m, pair_m, chip_m, chip_in, enter, factor, attn_s, osend,
    own_sem, send_sem, recv_sem, pair_sem, chip_send, chip_recv, out_send, out_recv,
):
    ctx, head = lax.axis_index("ctx"), lax.axis_index("head")
    tokens = k_ref.shape[0]
    group = tokens * nh
    chunk = E if group % E == 0 else group
    chunks = [(i * chunk, (i + 1) * chunk) for i in range(group // chunk)]
    chip, core = ctx // 2, ctx % 2
    sibling = ctx + 1 - 2 * core
    mesh_id = pl.DeviceIdType.MESH

    def columns(h):
        return pl.ds(pl.multiple_of(h * E, E), E)

    def quarter(h):
        return pl.ds(pl.multiple_of(h * tokens, tokens), tokens)

    local = (gl, kl, vl, ql)
    loads = [
        pltpu.make_async_copy(ref, buf, own_sem.at[a])
        for a, (ref, buf) in enumerate(zip((g_ref, k_ref, v_ref, q_ref), local))
    ]
    loads.append(pltpu.make_async_copy(gain_ref, gain_s, own_sem.at[4]))
    loads.append(pltpu.make_async_copy(ds_hbm, ds_ref, own_sem.at[5]))
    for copy in loads:
        copy.start()

    barrier = pltpu.get_barrier_semaphore()
    partners = [(ctx, lax.rem(head + d, nh)) for d in range(1, nh)] + [(sibling, head)]
    for partner in partners:
        pl.semaphore_signal(barrier, inc=1, device_id=partner, device_id_type=mesh_id)
    for d in range(1, nchip):
        @pl.when(chip >= d)
        def _():
            earlier = lax.rem(chip + nchip - d, nchip) * 2 + core
            pl.semaphore_signal(
                barrier, inc=1, device_id=(earlier, head), device_id_type=mesh_id
            )

    t_wide = lax.broadcasted_iota(jnp.int32, (group, group), 0)
    j_wide = lax.broadcasted_iota(jnp.int32, (group, group), 1)
    lower_s[...] = jnp.where(t_wide >= j_wide, 1.0, 0.0).astype(BF16)
    later_s[...] = jnp.where(t_wide > j_wide, 1.0, 0.0)

    for a in range(4):
        loads[a].wait()
    pl.semaphore_wait(barrier, len(partners) + nchip - 1 - chip)

    places = (gs, ks, vs, qs)

    def piece(a, h):
        return gl if a == 0 else local[a].at[:, columns(h)]

    def place(a, h):
        return gs.at[h] if a == 0 else places[a].at[quarter(h)]

    sends = {}
    for a in range(4):
        for d in range(1, nh):
            peer = lax.rem(head + d, nh)
            sends[a, d] = pltpu.make_async_remote_copy(
                src_ref=piece(a, peer), dst_ref=place(a, head),
                send_sem=send_sem.at[a, d - 1], recv_sem=recv_sem.at[a, d - 1],
                device_id=(ctx, peer), device_id_type=mesh_id,
            )
            sends[a, d].start()
    own = [
        pltpu.make_async_copy(piece(a, head), place(a, head), own_sem.at[6 + a])
        for a in range(4)
    ]
    for copy in own:
        copy.start()

    def arrived(a):
        own[a].wait()
        for d in range(1, nh):
            sends[a, d].wait_recv()

    loads[4].wait()
    loads[5].wait()
    offset = ctx * group
    ndoc = ds_ref.shape[0] - 1
    last_token = offset + group - 1
    t_pos = offset + lax.broadcasted_iota(jnp.int32, (group, E), 0)
    begun = jnp.zeros((group, E), jnp.int32)
    begun_last = jnp.int32(0)
    for m in range(ndoc):
        s = ds_ref[m]
        begun = jnp.where(t_pos >= s, s, begun)
        begun_last = jnp.where(last_token >= s, s, begun_last)

    arrived(0)
    ones = jnp.ones((gs.shape[1], E), BF16)
    row = lax.broadcasted_iota(jnp.int32, gs.shape[1:], 0)
    for t in range(nh):
        rows = jnp.where(row == head, gs[t].astype(F32), 0.0).astype(BF16)
        gcol[pl.ds(t * tokens, tokens), :] = dot(rows, ones, ((0,), (0,)))
    g_lanes = gcol[...]
    cum = dot(lower_s[...], g_lanes.astype(BF16))
    reach = jnp.exp(cum) * jnp.where(begun < offset, 1.0, 0.0)
    tail = jnp.exp(cum[group - 1 :, :] - cum) * jnp.where(t_pos >= begun_last, 1.0, 0.0)
    keep = reach[group - 1 :, :]
    for lo, hi in chunks:
        steps = (later_s[:hi, :hi] * g_lanes[:hi, :1]).astype(BF16)
        between = dot(lower_s[lo:hi, :hi], steps)
        t_at = lo + lax.broadcasted_iota(jnp.int32, (hi - lo, hi), 0)
        j_at = lax.broadcasted_iota(jnp.int32, (hi - lo, hi), 1)
        allowed = (j_at <= t_at) & (j_at + offset >= begun[lo:hi, :1])
        decay_s[lo:hi, :hi] = jnp.where(allowed, jnp.exp(between), 0.0)

    arrived(1)
    scaled = (ks[...].astype(F32) * tail).astype(BF16)
    arrived(2)
    summary = dot(scaled, vs[...], ((0,), (0,)))
    put_message(mine_m, summary, keep)
    to_pair = pltpu.make_async_remote_copy(
        src_ref=mine_m, dst_ref=pair_m, send_sem=pair_sem.at[0], recv_sem=pair_sem.at[1],
        device_id=(sibling, head), device_id_type=mesh_id,
    )
    to_pair.start()

    to_pair.wait_recv()
    pair_state, pair_keep = get_message(pair_m)
    first_core = core == 0
    total = jnp.where(
        first_core, pair_keep * summary + pair_state, keep * pair_state + summary
    )
    put_message(chip_m, total, pair_keep * keep)

    def to_chip(d):
        return pltpu.make_async_remote_copy(
            src_ref=chip_m, dst_ref=chip_in.at[d - 1],
            send_sem=chip_send.at[d - 1], recv_sem=chip_recv.at[d - 1],
            device_id=(lax.rem(chip + d, nchip) * 2 + core, head), device_id_type=mesh_id,
        )

    for d in range(1, nchip):
        @pl.when(chip + d < nchip)
        def _():
            to_chip(d).start()

    arrived(3)
    for lo, hi in chunks:
        scores = dot(qs[lo:hi, :], ks[:hi, :], ((1,), (1,)))
        weights = (scores * decay_s[lo:hi, :hi]).astype(BF16)
        attn_s[lo:hi, :] = dot(weights, vs[:hi, :])
    gcol[...] = reach

    enter[...] = jnp.zeros_like(enter)
    factor[...] = jnp.ones_like(factor)
    for d in range(1, nchip):
        @pl.when(chip >= d)
        def _():
            to_chip(d).wait_recv()
            state, held = get_message(chip_in.at[d - 1])
            enter[...] += factor[...] * state
            factor[...] = factor[...] * held
    state = enter[...]
    state = jnp.where(first_core, state, pair_keep * state + pair_state)
    state = state.astype(BF16)

    back = []
    for d in list(range(1, nh)) + [0]:
        peer = lax.rem(head + d, nh)
        rows = quarter(peer)
        q = qs[rows, :]
        attn = attn_s[rows, :] + gcol[rows, :] * dot(q, state)
        meansq = jnp.mean(attn * attn, axis=1, keepdims=True)
        osend[rows, :] = (attn * lax.rsqrt(meansq + 1e-05) * gain_s[...]).astype(BF16)
        if d:
            copy = pltpu.make_async_remote_copy(
                src_ref=osend.at[rows], dst_ref=o_ref.at[:, columns(head)],
                send_sem=out_send.at[d - 1], recv_sem=out_recv.at[d - 1],
                device_id=(ctx, peer), device_id_type=mesh_id,
            )
        else:
            copy = pltpu.make_async_copy(
                osend.at[rows], o_ref.at[:, columns(head)], own_sem.at[10]
            )
        copy.start()
        back.append(copy)

    to_pair.wait_send()
    for copy in sends.values():
        copy.wait_send()
    for d in range(1, nchip):
        @pl.when(chip + d < nchip)
        def _():
            to_chip(d).wait_send()
    for copy in back:
        copy.wait()


def in_hbm(x):
    return pltpu.with_memory_space_constraint(x, pltpu.HBM)


def fused_device(queries, keys, values, log_decay, gain, doc_starts):
    nh, nctx = lax.axis_size("head"), lax.axis_size("ctx")
    nchip = nctx // 2
    hops = max(nchip - 1, 1)
    tokens, width = queries.shape
    group = tokens * nh
    decays = log_decay.T
    hbm = pl.BlockSpec(memory_space=pltpu.HBM)
    dma = pltpu.SemaphoreType.DMA
    message = (E + KEEP_ROWS, E)
    return pl.pallas_call(
        functools.partial(fused, nh, nchip),
        out_shape=pltpu.VMEM(queries.shape, queries.dtype),
        in_specs=[hbm] * 6,
        out_specs=pl.BlockSpec(memory_space=pltpu.VMEM),
        scratch_shapes=[
            pltpu.VMEM((tokens, width), BF16),
            pltpu.VMEM((tokens, width), BF16),
            pltpu.VMEM((tokens, width), BF16),
            pltpu.VMEM(decays.shape, BF16),
            pltpu.SMEM(doc_starts.shape, jnp.int32),
            pltpu.VMEM((group, E), BF16),
            pltpu.VMEM((group, E), BF16),
            pltpu.VMEM((group, E), BF16),
            pltpu.VMEM((nh, *decays.shape), BF16),
            pltpu.VMEM((1, E), F32),
            pltpu.VMEM((group, group), BF16),
            pltpu.VMEM((group, group), F32),
            pltpu.VMEM((group, group), F32),
            pltpu.VMEM((group, E), F32),
            pltpu.VMEM(message, BF16),
            pltpu.VMEM(message, BF16),
            pltpu.VMEM(message, BF16),
            pltpu.VMEM((hops, *message), BF16),
            pltpu.VMEM((E, E), F32),
            pltpu.VMEM((1, E), F32),
            pltpu.VMEM((group, E), F32),
            pltpu.VMEM((group, E), BF16),
            dma((11,)),
            dma((4, nh - 1)),
            dma((4, nh - 1)),
            dma((2,)),
            dma((hops,)),
            dma((hops,)),
            dma((nh - 1,)),
            dma((nh - 1,)),
        ],
        compiler_params=pltpu.CompilerParams(
            collective_id=0, has_side_effects=True, vmem_limit_bytes=32 * 1024 * 1024
        ),
        cost_estimate=pl.CostEstimate(
            flops=2 * group * E * (2 * group + 3 * E) + 2 * group**3,
            bytes_accessed=8 * group * E,
            transcendentals=group * group,
        ),
    )(*map(in_hbm, (queries, keys, values, decays, gain.reshape(1, E), doc_starts)))


def per_device(queries, keys, values, log_decay, gain, doc_starts):
    nh, nctx = lax.axis_size("head"), lax.axis_size("ctx")
    tokens = queries.shape[0]
    one_block = tokens * nh <= block_cap and tokens % 16 == 0
    if one_block and gain.shape[0] == E and nh > 1 and nctx % 2 == 0:
        return fused_device(queries, keys, values, log_decay, gain, doc_starts)
    return scanned(queries, keys, values, log_decay, gain, doc_starts)


def solution(mesh):
    in_specs = (
        P(("ctx", "head"), None),
        P(("ctx", "head"), None),
        P(("ctx", "head"), None),
        P(("ctx", "head"), None),
        P("head"),
        P(),
    )
    out_specs = P(("ctx", "head"), None)
    return jax.shard_map(
        per_device, mesh=mesh, in_specs=in_specs, out_specs=out_specs, check_vma=False
    )
```
